256 devices in a mesh: seq: 64 (over x, z, y_lo), head: 4 (over y_hi, core).
Axes of the slice: x: 4, y: 4 (y_hi: 2, y_lo: 2; y = y_hi * 2 + y_lo), z: 8, core: 2. Of those that a mesh axis runs over, the one named last changes fastest.
Arguments:
- queries: bfloat16 [16384, 2048], P('seq', 'head'), may hold values from -150 to 150
- keys: bfloat16 [16384, 2048], P('seq', 'head'), may hold values from -6 to 6
- values: bfloat16 [16384, 2048], P('seq', 'head'), may hold values from -8 to 8
- out_grad: bfloat16 [16384, 2048], P(('seq', 'head')), may hold values from -96 to 96
Outputs:
- query_grad: bfloat16 [16384, 2048], P('seq', 'head')
- key_grad: bfloat16 [16384, 2048], P('seq', 'head')
- value_grad: bfloat16 [16384, 2048], P('seq', 'head')
The draws below stay inside these ranges and needn't reach their ends.
All inputs are finite; a program needn't handle non-finite values.
Results may differ from the reference program's by a relative error of at most 0.03.
Values may be sent and summed in bfloat16 or wider, within the bound.
A program may use at most 64 MiB of HBM per device.

```python
import jax
import jax.numpy as jnp
from jax import lax

HEADS = 16
HEAD_DIM = 128
STRIDE = 256
WIDTH = 2048
TOKENS = 16384


def shared_base(key):
    return jnp.clip(jax.random.normal(key, (TOKENS, WIDTH), jnp.float32), -6.0, 6.0)


def draw_queries(key, part):
    key = jax.random.fold_in(key, 7)
    own = jnp.clip(jax.random.normal(key, (TOKENS, WIDTH), jnp.float32), -6.0, 6.0)
    return own.astype(jnp.bfloat16)


def draw_keys(key, part):
    base = shared_base(key)
    return base.astype(jnp.bfloat16)


def draw_values(key, part):
    key = jax.random.fold_in(key, 13)
    own = jnp.clip(jax.random.normal(key, (TOKENS, WIDTH), jnp.float32), -6.0, 6.0)
    offset = jax.random.uniform(jax.random.fold_in(key, 2), (1, WIDTH), jnp.float32, -1.5, 1.5)
    return jnp.clip(own + offset, -8.0, 8.0).astype(jnp.bfloat16)


def shard_levels(key, dims, split, smallest, largest):
    gain, own = 1.0, jax.random.fold_in(key, 6)
    for position, shards_of in split:
        draws = jnp.exp(jax.random.uniform(jax.random.fold_in(own, position), (shards_of,), jnp.float32, smallest / len(split), largest / len(split)))
        gain = gain * jnp.repeat(draws, dims[position] // shards_of).reshape([-1 if axis == position else 1 for axis in range(len(dims))])
    return gain


def gaussian(key, extent, deviation, bound, split=(), dtype=jnp.bfloat16):
    factor_of = shard_levels(key, extent, split, -0.22, 0.18) if split else 1.0
    entries = jax.random.normal(key, extent, jnp.float32) * deviation * factor_of
    return jnp.minimum(jnp.maximum(entries, -bound), bound).astype(dtype)


def setup_inputs(seed: int = 0) -> dict:
    key_of = jax.random.split(jax.random.key(seed), 5)
    queries = draw_queries(jax.random.fold_in(key_of[4], 71), 0)
    keys = draw_keys(jax.random.fold_in(key_of[4], 71), 0)
    values = draw_values(jax.random.fold_in(key_of[4], 71), 0)
    out_grad = gaussian(key_of[3], (TOKENS, WIDTH), 16.0, 96.0, ((0, 256),))
    return {"queries": queries, "keys": keys, "values": values, "out_grad": out_grad}


NEG_LARGE = -1.0e30


def rounded_length(matrix):
    return lax.optimization_barrier(matrix.astype(jnp.bfloat16)).astype(jnp.float32)


def with_previous(blocks):
    empty = jnp.zeros((1,) + blocks.shape[1:], jnp.float32)
    return jnp.concatenate([jnp.concatenate([empty, blocks[:-1]], 0), blocks], 1)


def one_head(operands):
    query_all, key_all, value_all, grad_all = operands
    blocks = TOKENS // STRIDE
    padding_multiple = HEAD_DIM ** -0.5
    query_block_rows = query_all.reshape(blocks, STRIDE, HEAD_DIM)
    key_blk = key_all.reshape(blocks, STRIDE, HEAD_DIM)
    value_blk = value_all.reshape(blocks, STRIDE, HEAD_DIM)
    gradient_block_rows = grad_all.reshape(blocks, STRIDE, HEAD_DIM)
    extended_keys = with_previous(key_blk)
    extended_values = with_previous(value_blk)
    query_pos = jnp.arange(STRIDE)[:, None]
    key_pos = jnp.arange(2 * STRIDE)[None, :]
    inside = (key_pos > query_pos) & (key_pos <= query_pos + STRIDE)
    block_ids = jnp.arange(blocks)[:, None, None]
    band_ok = inside[None] & ((block_ids > 0) | (key_pos[None] >= STRIDE))
    local_score_matrix = jnp.einsum('xac,xhc->xah', query_block_rows, extended_keys) * padding_multiple
    local_score_matrix = jnp.where(band_ok, local_score_matrix, NEG_LARGE)
    band_max = jnp.max(local_score_matrix, -1)
    band_sum = jnp.sum(jnp.where(band_ok, jnp.exp(local_score_matrix - band_max[..., None]), 0.0), -1)
    query_cls = query_block_rows.transpose(1, 0, 2)
    key_cls = key_blk.transpose(1, 0, 2)
    value_cls = value_blk.transpose(1, 0, 2)
    grad_cls = gradient_block_rows.transpose(1, 0, 2)
    class_ok = jnp.arange(blocks)[None, :] < jnp.arange(blocks)[:, None]
    class_scores = jnp.einsum('rpd,rqd->rpq', query_cls, key_cls) * padding_multiple
    class_scores = jnp.where(class_ok[None], class_scores, NEG_LARGE)
    class_max = jnp.max(class_scores, -1)
    class_sum = jnp.sum(jnp.where(class_ok[None], jnp.exp(class_scores - class_max[..., None]), 0.0), -1)
    top = jnp.maximum(band_max, class_max.T)
    lse = top + jnp.log(band_sum * jnp.exp(band_max - top) + class_sum.T * jnp.exp(class_max.T - top))
    local_probabilities = jnp.where(band_ok, jnp.exp(local_score_matrix - lse[..., None]), 0.0)
    local_probability_gradient = jnp.einsum('xac,xhc->xah', gradient_block_rows, extended_values)
    class_probs = jnp.where(class_ok[None], jnp.exp(class_scores - lse.T[..., None]), 0.0)
    class_pgrad = jnp.einsum('rpd,rqd->rpq', grad_cls, value_cls)
    delta = jnp.sum(local_probabilities * local_probability_gradient, -1) + jnp.sum(class_probs * class_pgrad, -1).T
    local_score_gradient = rounded_length(local_probabilities * (local_probability_gradient - delta[..., None]))
    class_sgrad = rounded_length(class_probs * (class_pgrad - delta.T[..., None]))
    local_query_gradient = jnp.einsum('xjr,xro->xjo', local_score_gradient, extended_keys) * padding_multiple
    extended_key_gradient = jnp.einsum('yir,yiz->yrz', local_score_gradient, query_block_rows) * padding_multiple
    extended_value_gradient = jnp.einsum('yir,yiz->yrz', rounded_length(local_probabilities), gradient_block_rows)
    empty = jnp.zeros((1, STRIDE, HEAD_DIM), jnp.float32)
    band_dk = extended_key_gradient[:, STRIDE:] + jnp.concatenate([extended_key_gradient[1:, :STRIDE], empty], 0)
    band_dv = extended_value_gradient[:, STRIDE:] + jnp.concatenate([extended_value_gradient[1:, :STRIDE], empty], 0)
    class_dq = jnp.einsum('rpq,rqd->rpd', class_sgrad, key_cls) * padding_multiple
    class_dk = jnp.einsum('rpq,rpd->rqd', class_sgrad, query_cls) * padding_multiple
    class_dv = jnp.einsum('rpq,rpd->rqd', rounded_length(class_probs), grad_cls)
    grad_q = (local_query_gradient + class_dq.transpose(1, 0, 2)).reshape(TOKENS, HEAD_DIM)
    grad_k = (band_dk + class_dk.transpose(1, 0, 2)).reshape(TOKENS, HEAD_DIM)
    grad_v = (band_dv + class_dv.transpose(1, 0, 2)).reshape(TOKENS, HEAD_DIM)
    return grad_q, grad_k, grad_v


def by_heads(matrix):
    return matrix.astype(jnp.float32).reshape(TOKENS, HEADS, HEAD_DIM).transpose(1, 0, 2)


def from_heads(stacked):
    return stacked.transpose(1, 0, 2).reshape(TOKENS, HEADS * HEAD_DIM).astype(jnp.bfloat16)


def reference(queries, keys, values, out_grad):
    grad_q, grad_k, grad_v = lax.map(one_head, (by_heads(queries), by_heads(keys), by_heads(values), by_heads(out_grad)))
    return from_heads(grad_q), from_heads(grad_k), from_heads(grad_v)
```

```python
import functools

import jax
import jax.numpy as jnp
from jax import lax
from jax.experimental import pallas as pl
from jax.experimental.pallas import tpu as pltpu
from jax.sharding import PartitionSpec as P

HEAD_DIM = 128
STRIDE = 256
TILE = 16
NEG_LARGE = -1e30
SCALE = HEAD_DIM**-0.5
MESH = pl.DeviceIdType.MESH
F32 = jnp.float32
BF16 = jnp.bfloat16


def dot_nt(a, b):
    return lax.dot_general(a, b, (((1,), (1,)), ((), ())), preferred_element_type=F32)


def dot_nn(a, b):
    return lax.dot_general(a, b, (((1,), (0,)), ((), ())), preferred_element_type=F32)


def dot_tn(a, b):
    return lax.dot_general(a, b, (((0,), (0,)), ((), ())), preferred_element_type=F32)


def iota(shape, axis):
    return lax.broadcasted_iota(jnp.int32, shape, axis)


def kernel(
    seq_count, head_count,
    q_ref, k_ref, v_ref, og_ref,
    dq_ref, dk_ref, dv_ref,
    g_home, halo, back_snd, back_rcv,
    snd, rcv, gsnd, grcv, stat_snd, stat_rcv, cstat_snd, cstat_rcv, grad_snd, grad_rcv,
    wide, classes, gwide, e_diag, e_prev, pg_diag, pg_prev, stat_col, acc,
    g_send_sem, g_recv_sem, halo_send_sem, halo_recv_sem, back_send_sem, back_recv_sem,
    send_sem, recv_sem,
):
    s = lax.axis_index("seq")
    hd = lax.axis_index("head")
    others = seq_count - 1
    heads = q_ref.shape[1] // HEAD_DIM
    tiles = STRIDE // TILE
    width = q_ref.shape[1]
    after = lax.rem(s + 1, seq_count)
    before = lax.rem(s + seq_count - 1, seq_count)
    part = og_ref.shape[0]

    barrier = pltpu.get_barrier_semaphore()

    @pl.loop(1, seq_count)
    def _(i):
        pl.semaphore_signal(
            barrier, inc=1, device_id=(lax.rem(s + i, seq_count), hd), device_id_type=MESH
        )

    @pl.loop(1, head_count)
    def _(i):
        pl.semaphore_signal(
            barrier, inc=1, device_id=(s, lax.rem(hd + i, head_count)), device_id_type=MESH
        )

    for j, ref in enumerate((q_ref, k_ref, v_ref)):
        for h in range(heads):
            snd[h * tiles : (h + 1) * tiles, j] = ref[
                :, h * HEAD_DIM : (h + 1) * HEAD_DIM
            ].reshape(tiles, TILE, HEAD_DIM)
    own_rows = pl.ds(pl.multiple_of(hd * part, part), part)
    g_home[own_rows, :] = og_ref[:, pl.ds(pl.multiple_of(hd * width, width), width)]

    pl.semaphore_wait(barrier, others + head_count - 1)

    def send_all(src, dst, index):
        @pl.loop(1, seq_count)
        def _(i):
            peer = lax.rem(s + i, seq_count)
            pltpu.make_async_remote_copy(
                src_ref=src.at[peer],
                dst_ref=dst.at[s],
                send_sem=send_sem.at[index],
                recv_sem=recv_sem.at[index],
                device_id=(peer, hd),
                device_id_type=MESH,
            ).start()

    def whole(src, dst, index):
        return pltpu.make_async_remote_copy(
            src_ref=src.at[pl.ds(0, others)],
            dst_ref=dst.at[pl.ds(0, others)],
            send_sem=send_sem.at[index],
            recv_sem=recv_sem.at[index],
            device_id=(after, hd),
            device_id_type=MESH,
        )

    g_copies = []
    for i in range(1, head_count):
        peer = lax.rem(hd + i, head_count)
        copy = pltpu.make_async_remote_copy(
            src_ref=og_ref.at[:, pl.ds(pl.multiple_of(peer * width, width), width)],
            dst_ref=g_home.at[own_rows, :],
            send_sem=g_send_sem.at[i],
            recv_sem=g_recv_sem.at[i],
            device_id=(s, peer),
            device_id_type=MESH,
        )
        copy.start()
        g_copies.append(copy)
    halo_copies = []
    for j, ref in enumerate((k_ref, v_ref)):
        copy = pltpu.make_async_remote_copy(
            src_ref=ref,
            dst_ref=halo.at[j],
            send_sem=halo_send_sem.at[j],
            recv_sem=halo_recv_sem.at[j],
            device_id=(after, hd),
            device_id_type=MESH,
        )
        copy.start()
        halo_copies.append(copy)
    send_all(snd, rcv, 0)
    rcv[s] = snd[s]

    for copy in g_copies:
        copy.wait_recv()
    for h in range(heads):
        gsnd[h * tiles : (h + 1) * tiles] = g_home[
            :, h * HEAD_DIM : (h + 1) * HEAD_DIM
        ].reshape(tiles, TILE, HEAD_DIM)
    send_all(gsnd, grcv, 1)
    grcv[s] = gsnd[s]

    for copy in halo_copies:
        copy.wait_recv()

    row = iota((STRIDE, STRIDE), 0)
    col = iota((STRIDE, STRIDE), 1)
    lane = iota((STRIDE, HEAD_DIM), 1)
    row_in_tile = lax.rem(iota((STRIDE, HEAD_DIM), 0), TILE)

    @pl.loop(0, heads)
    def _(h):
        at = pl.ds(pl.multiple_of(h * HEAD_DIM, HEAD_DIM), HEAD_DIM)
        qh, gh = q_ref[:, at], g_home[:, at]
        sd = jnp.where(col <= row, dot_nt(qh, k_ref[:, at]) * SCALE, NEG_LARGE)
        sp = jnp.where((col > row) & (s > 0), dot_nt(qh, halo[0, :, at]) * SCALE, NEG_LARGE)
        top = jnp.maximum(
            jnp.max(sd, axis=1, keepdims=True), jnp.max(sp, axis=1, keepdims=True)
        )
        ed, ep = jnp.exp(sd - top), jnp.exp(sp - top)
        gd, gp = dot_nt(gh, v_ref[:, at]), dot_nt(gh, halo[1, :, at])
        total = jnp.sum(ed, axis=1, keepdims=True) + jnp.sum(ep, axis=1, keepdims=True)
        weighted = jnp.sum(ed * gd, axis=1, keepdims=True) + jnp.sum(
            ep * gp, axis=1, keepdims=True
        )
        e_diag[h], e_prev[h], pg_diag[h], pg_prev[h] = ed, ep, gd, gp
        stat_col[h] = jnp.where(lane == 0, top, jnp.where(lane == 1, total, weighted))
        spread = jnp.where(
            lane == row_in_tile,
            top,
            jnp.where(
                lane == row_in_tile + TILE,
                total,
                jnp.where(lane == row_in_tile + 2 * TILE, weighted, 0.0),
            ),
        )
        stat_snd[pl.ds(pl.multiple_of(h * tiles, tiles), tiles), 0, :] = jnp.sum(
            spread.reshape(tiles, TILE, HEAD_DIM), axis=1
        )

    send_all(stat_snd, stat_rcv, 2)
    stat_rcv[s] = stat_snd[s]

    whole(snd, rcv, 0).wait_recv()
    whole(gsnd, grcv, 1).wait_recv()
    for j in range(4):
        block = rcv[:, j] if j < 3 else grcv[...]
        wide[j] = block.reshape(seq_count * TILE, HEAD_DIM).astype(F32)
    for j in range(4):
        for r in range(TILE):
            classes[j, r * seq_count : (r + 1) * seq_count, :] = wide[
                j, pl.ds(r, seq_count, stride=TILE), :
            ].astype(BF16)
    whole(stat_snd, stat_rcv, 2).wait_recv()
    band = stat_rcv[:, 0, :]

    pair = 2 * seq_count
    prow = iota((pair, pair), 0)
    pcol = iota((pair, pair), 1)
    allowed = ((prow < seq_count) == (pcol < seq_count)) & (pcol < prow)
    slane = iota((seq_count, HEAD_DIM), 1)
    stats = jnp.zeros((seq_count, HEAD_DIM), F32)
    for p in range(TILE // 2):
        rows = slice(p * pair, (p + 1) * pair)
        cq, ck, cv, cg = (classes[j, rows, :] for j in range(4))
        sc = jnp.where(allowed, dot_nt(cq, ck) * SCALE, NEG_LARGE)
        top = jnp.max(sc, axis=1, keepdims=True)
        ec = jnp.where(allowed, jnp.exp(sc - top), 0.0)
        pg = dot_nt(cg, cv)
        total = jnp.sum(ec, axis=1, keepdims=True)
        weighted = jnp.sum(ec * pg, axis=1, keepdims=True)
        for c in range(2):
            r = 2 * p + c
            half = slice(c * seq_count, (c + 1) * seq_count)
            for n, value in enumerate((top, total, weighted)):
                stats = jnp.where(slane == n * TILE + r, value[half], stats)
        b_top, b_total, b_weighted = (
            jnp.concatenate(
                [band[:, n * TILE + 2 * p + c : n * TILE + 2 * p + c + 1] for c in range(2)], axis=0
            )
            for n in range(3)
        )
        peak = jnp.maximum(top, b_top)
        f_class, f_band = jnp.exp(top - peak), jnp.exp(b_top - peak)
        inverse = 1.0 / (total * f_class + b_total * f_band)
        delta = (weighted * f_class + b_weighted * f_band) * inverse
        probs = ec * (f_class * inverse)
        sgrad = (probs * (pg - delta)).astype(BF16)
        grads = (
            dot_nn(sgrad, ck) * SCALE,
            dot_tn(sgrad, cq) * SCALE,
            dot_tn(probs.astype(BF16), cg),
        )
        for j in range(3):
            for c in range(2):
                gwide[j, pl.ds(2 * p + c, seq_count, stride=TILE), :] = grads[j][
                    c * seq_count : (c + 1) * seq_count
                ]
    cstat_snd[:, 0, :] = stats
    send_all(cstat_snd, cstat_rcv, 3)
    cstat_rcv[s] = cstat_snd[s]
    for j in range(3):
        grad_snd[:, j] = gwide[j].reshape(seq_count, TILE, HEAD_DIM).astype(BF16)
    send_all(grad_snd, grad_rcv, 4)
    grad_rcv[s] = grad_snd[s]

    whole(cstat_snd, cstat_rcv, 3).wait_recv()

    @pl.loop(0, heads)
    def _(h):
        at = pl.ds(pl.multiple_of(h * HEAD_DIM, HEAD_DIM), HEAD_DIM)
        got = cstat_rcv[pl.ds(pl.multiple_of(h * tiles, tiles), tiles), 0, :]
        got = jnp.broadcast_to(got[:, None, :], (tiles, TILE, HEAD_DIM)).reshape(
            STRIDE, HEAD_DIM
        )
        c_top, c_total, c_weighted = (
            jnp.sum(
                jnp.where(lane == row_in_tile + n * TILE, got, 0.0), axis=1, keepdims=True
            )
            for n in range(3)
        )
        own = stat_col[h]
        top, total, weighted = own[:, 0:1], own[:, 1:2], own[:, 2:3]
        peak = jnp.maximum(top, c_top)
        f_class, f_band = jnp.exp(c_top - peak), jnp.exp(top - peak)
        inverse = 1.0 / (c_total * f_class + total * f_band)
        delta = (c_weighted * f_class + weighted * f_band) * inverse
        factor = f_band * inverse
        pd, pp = e_diag[h] * factor, e_prev[h] * factor
        sd = (pd * (pg_diag[h] - delta)).astype(BF16)
        sp = (pp * (pg_prev[h] - delta)).astype(BF16)
        qh, gh = q_ref[:, at], g_home[:, at]
        back_snd[0, :, at] = (dot_tn(sp, qh) * SCALE).astype(BF16)
        back_snd[1, :, at] = dot_tn(pp.astype(BF16), gh).astype(BF16)
        acc[0, :, at] = (dot_nn(sd, k_ref[:, at]) + dot_nn(sp, halo[0, :, at])) * SCALE
        acc[1, :, at] = dot_tn(sd, qh) * SCALE
        acc[2, :, at] = dot_tn(pd.astype(BF16), gh)

    back = pltpu.make_async_remote_copy(
        src_ref=back_snd,
        dst_ref=back_rcv,
        send_sem=back_send_sem,
        recv_sem=back_recv_sem,
        device_id=(before, hd),
        device_id_type=MESH,
    )
    back.start()
    whole(grad_snd, grad_rcv, 4).wait_recv()
    back.wait_recv()
    for h in range(heads):
        at = slice(h * HEAD_DIM, (h + 1) * HEAD_DIM)
        for j, out in enumerate((dq_ref, dk_ref, dv_ref)):
            value = acc[j, :, at] + grad_rcv[h * tiles : (h + 1) * tiles, j].reshape(
                STRIDE, HEAD_DIM
            ).astype(F32)
            if j > 0:
                value = value + back_rcv[j - 1, :, at].astype(F32)
            out[:, at] = value.astype(BF16)

    for copy in g_copies + halo_copies:
        copy.wait_send()
    for index, buffers in enumerate(
        ((snd, rcv), (gsnd, grcv), (stat_snd, stat_rcv), (cstat_snd, cstat_rcv), (grad_snd, grad_rcv))
    ):
        whole(*buffers, index).wait_send()
    back.wait_send()


def per_device(queries, keys, values, out_grad):
    length, width = queries.shape
    seq_count = lax.axis_size("seq")
    head_count = lax.axis_size("head")
    heads = width // HEAD_DIM
    assert length == STRIDE and seq_count * TILE == STRIDE * heads
    vmem = pl.BlockSpec(memory_space=pltpu.VMEM)
    tile = (TILE, HEAD_DIM)
    return pl.pallas_call(
        functools.partial(kernel, seq_count, head_count),
        out_shape=[jax.ShapeDtypeStruct(queries.shape, BF16)] * 3,
        in_specs=[vmem] * 4,
        out_specs=[vmem] * 3,
        scratch_shapes=[
            pltpu.VMEM((length, width), BF16),
            pltpu.VMEM((2, length, width), BF16),
            pltpu.VMEM((2, length, width), BF16),
            pltpu.VMEM((2, length, width), BF16),
            pltpu.VMEM((seq_count, 3) + tile, BF16),
            pltpu.VMEM((seq_count, 3) + tile, BF16),
            pltpu.VMEM((seq_count,) + tile, BF16),
            pltpu.VMEM((seq_count,) + tile, BF16),
            pltpu.VMEM((seq_count, 1, HEAD_DIM), F32),
            pltpu.VMEM((seq_count, 1, HEAD_DIM), F32),
            pltpu.VMEM((seq_count, 1, HEAD_DIM), F32),
            pltpu.VMEM((seq_count, 1, HEAD_DIM), F32),
            pltpu.VMEM((seq_count, 3) + tile, BF16),
            pltpu.VMEM((seq_count, 3) + tile, BF16),
            pltpu.VMEM((4, seq_count * TILE, HEAD_DIM), F32),
            pltpu.VMEM((4, seq_count * TILE, HEAD_DIM), BF16),
            pltpu.VMEM((3, seq_count * TILE, HEAD_DIM), F32),
            pltpu.VMEM((heads, STRIDE, STRIDE), F32),
            pltpu.VMEM((heads, STRIDE, STRIDE), F32),
            pltpu.VMEM((heads, STRIDE, STRIDE), F32),
            pltpu.VMEM((heads, STRIDE, STRIDE), F32),
            pltpu.VMEM((heads, STRIDE, HEAD_DIM), F32),
            pltpu.VMEM((3, length, width), F32),
            pltpu.SemaphoreType.DMA((head_count,)),
            pltpu.SemaphoreType.DMA((head_count,)),
            pltpu.SemaphoreType.DMA((2,)),
            pltpu.SemaphoreType.DMA((2,)),
            pltpu.SemaphoreType.DMA,
            pltpu.SemaphoreType.DMA,
            pltpu.SemaphoreType.DMA((5,)),
            pltpu.SemaphoreType.DMA((5,)),
        ],
        compiler_params=pltpu.CompilerParams(
            collective_id=0, has_side_effects=True, vmem_limit_bytes=48 * 2**20
        ),
    )(queries, keys, values, out_grad)


def solution(mesh):
    return jax.shard_map(
        per_device,
        mesh=mesh,
        in_specs=(P("seq", "head"), P("seq", "head"), P("seq", "head"), P(("seq", "head"), None)),
        out_specs=(P("seq", "head"), P("seq", "head"), P("seq", "head")),
        check_vma=False,
    )
```

```python
import functools

import jax
import jax.numpy as jnp
from jax import lax
from jax.experimental import pallas as pl
from jax.experimental.pallas import tpu as pltpu
from jax.sharding import PartitionSpec as P

HEAD_DIM = 128
STRIDE = 256
TILE = 16
PAIRS = TILE // 2
HALF = 32
NEG_LARGE = -1e30
SCALE = HEAD_DIM**-0.5
STEP = 1
EARLY = 40
MESH = pl.DeviceIdType.MESH
F32 = jnp.float32
BF16 = jnp.bfloat16


def dot_nt(a, b):
    return lax.dot_general(a, b, (((1,), (1,)), ((), ())), preferred_element_type=F32)


def dot_nn(a, b):
    return lax.dot_general(a, b, (((1,), (0,)), ((), ())), preferred_element_type=F32)


def dot_tn(a, b):
    return lax.dot_general(a, b, (((0,), (0,)), ((), ())), preferred_element_type=F32)


def dot_exact(a, b):
    return lax.dot_general(
        a, b, (((1,), (0,)), ((), ())),
        preferred_element_type=F32, precision=lax.Precision.HIGHEST,
    )


def iota(shape, axis):
    return lax.broadcasted_iota(jnp.int32, shape, axis)


def combine(top, total, weighted, other_top, other_total, other_weighted):
    peak = jnp.maximum(top, other_top)
    mine, theirs = jnp.exp(top - peak), jnp.exp(other_top - peak)
    inverse = 1.0 / (total * mine + other_total * theirs)
    return mine * inverse, (weighted * mine + other_weighted * theirs) * inverse


def kernel(
    seq_count, head_count,
    q_hbm, k_hbm, v_hbm, og_hbm,
    dq_ref, dk_ref, dv_ref,
    q_ref, kv_ref, og_ref, g_home, halo, back_snd, back_rcv,
    snd, rcv, gsnd, grcv, stat_snd, stat_rcv, cstat_snd, cstat_rcv, grad_snd, grad_rcv,
    classes, class_grad, class_e, class_pg, class_row,
    e_diag, e_prev, pg_diag, pg_prev, stat_row, cstat_row, acc,
    load_sem, g_send_sem, g_recv_sem, halo_send_sem, halo_recv_sem, back_send_sem, back_recv_sem,
    send_sem, recv_sem,
):
    s = lax.axis_index("seq")
    hd = lax.axis_index("head")
    others = seq_count - 1
    width = q_ref.shape[1]
    heads = width // HEAD_DIM
    tiles = STRIDE // TILE
    chunks = seq_count // TILE
    after = lax.rem(s + 1, seq_count)
    before = lax.rem(s + seq_count - 1, seq_count)
    part = og_ref.shape[0]

    loads = [
        pltpu.make_async_copy(src, dst, load_sem.at[i])
        for i, (src, dst) in enumerate(
            ((q_hbm, q_ref), (k_hbm, kv_ref.at[0]), (v_hbm, kv_ref.at[1]), (og_hbm, og_ref))
        )
    ]
    for load in loads:
        load.start()

    barrier = pltpu.get_barrier_semaphore()

    @pl.loop(1, seq_count)
    def _(i):
        pl.semaphore_signal(
            barrier, inc=1, device_id=(lax.rem(s + i, seq_count), hd), device_id_type=MESH
        )

    @pl.loop(1, head_count)
    def _(i):
        pl.semaphore_signal(
            barrier, inc=1, device_id=(s, lax.rem(hd + i, head_count)), device_id_type=MESH
        )

    for load in loads:
        load.wait()
    for j, ref in enumerate((q_ref, kv_ref.at[0], kv_ref.at[1])):
        for h in range(heads):
            snd[h * tiles : (h + 1) * tiles, j] = ref[
                :, h * HEAD_DIM : (h + 1) * HEAD_DIM
            ].reshape(tiles, TILE, HEAD_DIM)
    rcv[s] = snd[s]
    own_rows = pl.ds(pl.multiple_of(hd * part, part), part)
    g_home[own_rows, :] = og_ref[:, pl.ds(pl.multiple_of(hd * width, width), width)]

    pl.semaphore_wait(barrier, others + head_count - 1)

    def send(src, dst, index, i):
        peer = lax.rem(s + i * STEP, seq_count)
        pltpu.make_async_remote_copy(
            src_ref=src.at[peer],
            dst_ref=dst.at[s],
            send_sem=send_sem.at[index],
            recv_sem=recv_sem.at[index],
            device_id=(peer, hd),
            device_id_type=MESH,
        ).start()

    def whole(src, dst, index):
        return pltpu.make_async_remote_copy(
            src_ref=src.at[pl.ds(0, others)],
            dst_ref=dst.at[pl.ds(0, others)],
            send_sem=send_sem.at[index],
            recv_sem=recv_sem.at[index],
            device_id=(after, hd),
            device_id_type=MESH,
        )

    def strip(src, dst, send, recv, peer, i):
        rows = pl.ds(pl.multiple_of(i * TILE, TILE), TILE)
        pltpu.make_async_remote_copy(
            src_ref=src.at[:, rows, :],
            dst_ref=dst.at[:, rows, :],
            send_sem=send,
            recv_sem=recv,
            device_id=(peer, hd),
            device_id_type=MESH,
        ).start()

    def strips(src, dst, send, recv, peer):
        return pltpu.make_async_remote_copy(
            src_ref=src, dst_ref=dst, send_sem=send, recv_sem=recv,
            device_id=(peer, hd), device_id_type=MESH,
        )

    g_copies = []
    for i in range(1, head_count):
        peer = lax.rem(hd + i, head_count)
        copy = pltpu.make_async_remote_copy(
            src_ref=og_ref.at[:, pl.ds(pl.multiple_of(peer * width, width), width)],
            dst_ref=g_home.at[own_rows, :],
            send_sem=g_send_sem.at[i],
            recv_sem=g_recv_sem.at[i],
            device_id=(s, peer),
            device_id_type=MESH,
        )
        copy.start()
        g_copies.append(copy)

    @pl.loop(0, tiles)
    def _(i):
        strip(kv_ref, halo, halo_send_sem, halo_recv_sem, after, i)
        for n in range(4):
            if n < 3:
                send(snd, rcv, 0, 1 + i * 3 + n)

    @pl.loop(1 + 3 * tiles, seq_count)
    def _(i):
        send(snd, rcv, 0, i)

    for copy in g_copies:
        copy.wait_recv()
    for h in range(heads):
        gsnd[h * tiles : (h + 1) * tiles] = g_home[
            :, h * HEAD_DIM : (h + 1) * HEAD_DIM
        ].reshape(tiles, TILE, HEAD_DIM)

    @pl.loop(1, seq_count)
    def _(i):
        send(gsnd, grcv, 1, i)

    grcv[s] = gsnd[s]

    strips(kv_ref, halo, halo_send_sem, halo_recv_sem, after).wait_recv()

    row = iota((STRIDE, STRIDE), 0)
    col = iota((STRIDE, STRIDE), 1)

    @pl.loop(0, heads)
    def _(h):
        at = pl.ds(pl.multiple_of(h * HEAD_DIM, HEAD_DIM), HEAD_DIM)
        qh, gh = q_ref[:, at], g_home[:, at]
        sd = jnp.where(row <= col, dot_nt(kv_ref[0, :, at], qh) * SCALE, NEG_LARGE)
        sp = jnp.where((row > col) & (s > 0), dot_nt(halo[0, :, at], qh) * SCALE, NEG_LARGE)
        top = jnp.maximum(
            jnp.max(sd, axis=0, keepdims=True), jnp.max(sp, axis=0, keepdims=True)
        )
        ed, ep = jnp.exp(sd - top), jnp.exp(sp - top)
        gd, gp = dot_nt(kv_ref[1, :, at], gh), dot_nt(halo[1, :, at], gh)
        e_diag[h], e_prev[h], pg_diag[h], pg_prev[h] = ed, ep, gd, gp
        total = jnp.sum(ed + ep, axis=0, keepdims=True)
        weighted = jnp.sum(ed * gd + ep * gp, axis=0, keepdims=True)
        for n, value in enumerate((top, total, weighted)):
            stat_row[n, pl.ds(h, 1), :] = value

    owner = lax.rem(iota((seq_count, STRIDE), 0), tiles) == iota((seq_count, STRIDE), 1) // TILE
    code_row = lax.rem(iota((STRIDE, HEAD_DIM), 0), TILE)
    code_row = lax.rem(code_row, 2) * HALF + code_row // 2
    pick_lane = iota((STRIDE, HEAD_DIM), 1)
    code_col = lax.rem(iota((HEAD_DIM, STRIDE), 1), TILE)
    code_col = lax.rem(code_col, 2) * HALF + code_col // 2
    pick_row = iota((HEAD_DIM, STRIDE), 0)

    coded = jnp.zeros((seq_count, HEAD_DIM), F32)
    for n in range(3):
        values = jnp.broadcast_to(
            stat_row[n][:, None, :], (heads, tiles, STRIDE)
        ).reshape(seq_count, STRIDE)
        select = (pick_lane == code_row + n * PAIRS).astype(F32)
        coded = coded + dot_exact(jnp.where(owner, values, 0.0), select)
    stat_snd[:, 0, :] = coded
    stat_rcv[s] = stat_snd[s]

    @pl.loop(1, seq_count)
    def _(i):
        send(stat_snd, stat_rcv, 2, i)

    swap_row = iota((STRIDE, STRIDE), 0)
    swap_col = iota((STRIDE, STRIDE), 1)
    swap = (
        (swap_row // TILE == lax.rem(swap_col, TILE))
        & (lax.rem(swap_row, TILE) == swap_col // TILE)
    ).astype(BF16)

    whole(snd, rcv, 0).wait_recv()
    whole(gsnd, grcv, 1).wait_recv()
    for c in range(chunks):
        these = slice(c * TILE, (c + 1) * TILE)
        mixed = jnp.concatenate(
            [rcv[these, j].reshape(STRIDE, HEAD_DIM) for j in range(3)]
            + [grcv[these].reshape(STRIDE, HEAD_DIM)],
            axis=1,
        )
        sorted_rows = dot_nn(swap, mixed).astype(BF16)
        for j in range(4):
            classes[j, :, these, :] = sorted_rows[:, j * HEAD_DIM : (j + 1) * HEAD_DIM].reshape(
                TILE, TILE, HEAD_DIM
            )

    pair = 2 * seq_count
    prow = iota((pair, pair), 0)
    pcol = iota((pair, pair), 1)
    allowed = ((prow < seq_count) == (pcol < seq_count)) & (prow < pcol)

    def pair_of(j, p):
        return classes[j, 2 * p : 2 * p + 2].reshape(pair, HEAD_DIM)

    class_row[...] = jnp.zeros_like(class_row)
    for p in range(PAIRS):
        sc = jnp.where(allowed, dot_nt(pair_of(1, p), pair_of(0, p)) * SCALE, NEG_LARGE)
        pg = dot_nt(pair_of(2, p), pair_of(3, p))
        top = jnp.max(sc, axis=0, keepdims=True)
        ec = jnp.where(allowed, jnp.exp(sc - top), 0.0)
        class_e[p], class_pg[p] = ec, pg
        total = jnp.sum(ec, axis=0, keepdims=True)
        weighted = jnp.sum(ec * pg, axis=0, keepdims=True)
        for n, value in enumerate((top, total, weighted)):
            class_row[n * PAIRS + p : n * PAIRS + p + 1, :] = value
    columns = class_row[...].T
    small = iota((seq_count, HEAD_DIM), 1) < HALF
    cstat_snd[:, 0, :] = jnp.where(
        small, columns[:seq_count], pltpu.roll(columns[seq_count:], HALF, 1)
    )
    cstat_rcv[s] = cstat_snd[s]

    @pl.loop(1, seq_count)
    def _(i):
        send(cstat_snd, cstat_rcv, 3, i)

    whole(stat_snd, stat_rcv, 2).wait_recv()
    band = stat_rcv[:, 0, :]
    band_row = jnp.concatenate([band, pltpu.roll(band, HEAD_DIM - HALF, 1)], axis=0).T
    for p in range(PAIRS):
        factor, delta = combine(
            *(class_row[n * PAIRS + p : n * PAIRS + p + 1, :] for n in range(3)),
            *(band_row[n * PAIRS + p : n * PAIRS + p + 1, :] for n in range(3)),
        )
        probs = class_e[p] * factor
        sgrad = (probs * (class_pg[p] - delta)).astype(BF16)
        for j, value in enumerate(
            (
                dot_tn(sgrad, pair_of(1, p)) * SCALE,
                dot_nn(sgrad, pair_of(0, p)) * SCALE,
                dot_nn(probs.astype(BF16), pair_of(3, p)),
            )
        ):
            class_grad[j, 2 * p : 2 * p + 2] = value.astype(BF16).reshape(
                2, seq_count, HEAD_DIM
            )
    for c in range(chunks):
        these = slice(c * TILE, (c + 1) * TILE)
        mixed = jnp.concatenate(
            [class_grad[j, :, these, :].reshape(STRIDE, HEAD_DIM) for j in range(3)], axis=1
        )
        sorted_rows = dot_nn(swap, mixed).astype(BF16)
        for j in range(3):
            grad_snd[these, j] = sorted_rows[:, j * HEAD_DIM : (j + 1) * HEAD_DIM].reshape(
                TILE, TILE, HEAD_DIM
            )
    grad_rcv[s] = grad_snd[s]

    @pl.loop(1, EARLY)
    def _(i):
        send(grad_snd, grad_rcv, 4, i)

    whole(cstat_snd, cstat_rcv, 3).wait_recv()
    got = cstat_rcv[:, 0, :]
    for n in range(3):
        select = (pick_row == code_col + n * PAIRS).astype(F32)
        cstat_row[n] = jnp.sum(
            jnp.where(owner, dot_exact(got, select), 0.0).reshape(heads, tiles, STRIDE), axis=1
        )

    @pl.loop(0, heads)
    def _(h):
        at = pl.ds(pl.multiple_of(h * HEAD_DIM, HEAD_DIM), HEAD_DIM)
        factor, delta = combine(
            *(stat_row[n, pl.ds(h, 1), :] for n in range(3)),
            *(cstat_row[n, pl.ds(h, 1), :] for n in range(3)),
        )
        stat_row[0, pl.ds(h, 1), :] = factor
        stat_row[1, pl.ds(h, 1), :] = delta
        probs = e_prev[h] * factor
        sgrad = (probs * (pg_prev[h] - delta)).astype(BF16)
        back_snd[0, :, at] = (dot_nn(sgrad, q_ref[:, at]) * SCALE).astype(BF16)
        back_snd[1, :, at] = dot_nn(probs.astype(BF16), g_home[:, at]).astype(BF16)
        acc[0, :, at] = dot_tn(sgrad, halo[0, :, at])

    @pl.loop(0, tiles)
    def _(i):
        strip(back_snd, back_rcv, back_send_sem, back_recv_sem, before, i)
        send(grad_snd, grad_rcv, 4, EARLY + i)

    @pl.loop(EARLY + tiles, seq_count)
    def _(i):
        send(grad_snd, grad_rcv, 4, i)

    @pl.loop(0, heads)
    def _(h):
        at = pl.ds(pl.multiple_of(h * HEAD_DIM, HEAD_DIM), HEAD_DIM)
        factor, delta = (stat_row[n, pl.ds(h, 1), :] for n in range(2))
        probs = e_diag[h] * factor
        sgrad = (probs * (pg_diag[h] - delta)).astype(BF16)
        acc[0, :, at] = (acc[0, :, at] + dot_tn(sgrad, kv_ref[0, :, at])) * SCALE
        acc[1, :, at] = dot_nn(sgrad, q_ref[:, at]) * SCALE
        acc[2, :, at] = dot_nn(probs.astype(BF16), g_home[:, at])

    whole(grad_snd, grad_rcv, 4).wait_recv()
    back = strips(back_snd, back_rcv, back_send_sem, back_recv_sem, before)
    back.wait_recv()
    for h in range(heads):
        at = slice(h * HEAD_DIM, (h + 1) * HEAD_DIM)
        for j, out in enumerate((dq_ref, dk_ref, dv_ref)):
            value = acc[j, :, at] + grad_rcv[h * tiles : (h + 1) * tiles, j].reshape(
                STRIDE, HEAD_DIM
            ).astype(F32)
            if j > 0:
                value = value + back_rcv[j - 1, :, at].astype(F32)
            out[:, at] = value.astype(BF16)

    for copy in g_copies:
        copy.wait_send()
    strips(kv_ref, halo, halo_send_sem, halo_recv_sem, after).wait_send()
    for index, buffers in enumerate(
        ((snd, rcv), (gsnd, grcv), (stat_snd, stat_rcv), (cstat_snd, cstat_rcv), (grad_snd, grad_rcv))
    ):
        whole(*buffers, index).wait_send()
    back.wait_send()


def per_device(queries, keys, values, out_grad):
    length, width = queries.shape
    seq_count = lax.axis_size("seq")
    head_count = lax.axis_size("head")
    heads = width // HEAD_DIM
    assert length == STRIDE and seq_count * TILE == STRIDE * heads and seq_count * 2 == HEAD_DIM
    vmem = pl.BlockSpec(memory_space=pltpu.VMEM)
    far = pl.BlockSpec(memory_space=pltpu.HBM)
    tile = (TILE, HEAD_DIM)
    pair = 2 * seq_count
    return pl.pallas_call(
        functools.partial(kernel, seq_count, head_count),
        out_shape=[jax.ShapeDtypeStruct(queries.shape, BF16)] * 3,
        in_specs=[far] * 4,
        out_specs=[vmem] * 3,
        scratch_shapes=[
            pltpu.VMEM((length, width), BF16),
            pltpu.VMEM((2, length, width), BF16),
            pltpu.VMEM(out_grad.shape, BF16),
            pltpu.VMEM((length, width), BF16),
            pltpu.VMEM((2, length, width), BF16),
            pltpu.VMEM((2, length, width), BF16),
            pltpu.VMEM((2, length, width), BF16),
            pltpu.VMEM((seq_count, 3) + tile, BF16),
            pltpu.VMEM((seq_count, 3) + tile, BF16),
            pltpu.VMEM((seq_count,) + tile, BF16),
            pltpu.VMEM((seq_count,) + tile, BF16),
            pltpu.VMEM((seq_count, 1, HEAD_DIM), F32),
            pltpu.VMEM((seq_count, 1, HEAD_DIM), F32),
            pltpu.VMEM((seq_count, 1, HEAD_DIM), F32),
            pltpu.VMEM((seq_count, 1, HEAD_DIM), F32),
            pltpu.VMEM((seq_count, 3) + tile, BF16),
            pltpu.VMEM((seq_count, 3) + tile, BF16),
            pltpu.VMEM((4, TILE, seq_count, HEAD_DIM), BF16),
            pltpu.VMEM((3, TILE, seq_count, HEAD_DIM), BF16),
            pltpu.VMEM((PAIRS, pair, pair), F32),
            pltpu.VMEM((PAIRS, pair, pair), F32),
            pltpu.VMEM((HEAD_DIM, HEAD_DIM), F32),
            pltpu.VMEM((heads, STRIDE, STRIDE), F32),
            pltpu.VMEM((heads, STRIDE, STRIDE), F32),
            pltpu.VMEM((heads, STRIDE, STRIDE), F32),
            pltpu.VMEM((heads, STRIDE, STRIDE), F32),
            pltpu.VMEM((3, heads, STRIDE), F32),
            pltpu.VMEM((3, heads, STRIDE), F32),
            pltpu.VMEM((3, length, width), F32),
            pltpu.SemaphoreType.DMA((4,)),
            pltpu.SemaphoreType.DMA((head_count,)),
            pltpu.SemaphoreType.DMA((head_count,)),
            pltpu.SemaphoreType.DMA,
            pltpu.SemaphoreType.DMA,
            pltpu.SemaphoreType.DMA,
            pltpu.SemaphoreType.DMA,
            pltpu.SemaphoreType.DMA((5,)),
            pltpu.SemaphoreType.DMA((5,)),
        ],
        compiler_params=pltpu.CompilerParams(
            collective_id=0, has_side_effects=True, vmem_limit_bytes=62 * 2**20
        ),
    )(queries, keys, values, out_grad)


def solution(mesh):
    return jax.shard_map(
        per_device,
        mesh=mesh,
        in_specs=(P("seq", "head"), P("seq", "head"), P("seq", "head"), P(("seq", "head"), None)),
        out_specs=(P("seq", "head"), P("seq", "head"), P("seq", "head")),
        check_vma=False,
    )
```

```python
import functools

import jax
import jax.numpy as jnp
from jax import lax
from jax.experimental import pallas as pl
from jax.experimental.pallas import tpu as pltpu
from jax.sharding import PartitionSpec as P

HEAD_DIM = 128
STRIDE = 256
TILE = 16
PAIRS = TILE // 2
HALF = 32
NEG_LARGE = -1e30
SCALE = HEAD_DIM**-0.5
EARLY = 40
LAG = 3
MESH = pl.DeviceIdType.MESH
F32 = jnp.float32
BF16 = jnp.bfloat16


def dot_nt(a, b):
    return lax.dot_general(a, b, (((1,), (1,)), ((), ())), preferred_element_type=F32)


def dot_nn(a, b):
    return lax.dot_general(a, b, (((1,), (0,)), ((), ())), preferred_element_type=F32)


def dot_tn(a, b):
    return lax.dot_general(a, b, (((0,), (0,)), ((), ())), preferred_element_type=F32)


def dot_exact(a, b):
    return lax.dot_general(
        a, b, (((1,), (0,)), ((), ())),
        preferred_element_type=F32, precision=lax.Precision.HIGHEST,
    )


def iota(shape, axis):
    return lax.broadcasted_iota(jnp.int32, shape, axis)


def combine(top, total, weighted, other_top, other_total, other_weighted):
    peak = jnp.maximum(top, other_top)
    mine, theirs = jnp.exp(top - peak), jnp.exp(other_top - peak)
    inverse = 1.0 / (total * mine + other_total * theirs)
    return mine * inverse, (weighted * mine + other_weighted * theirs) * inverse


def kernel(
    seq_count, head_count,
    q_hbm, k_hbm, v_hbm, og_hbm,
    dq_ref, dk_ref, dv_ref,
    q_ref, kv_ref, og_ref, g_home, halo, relay, back_snd, back_rcv, back_relay,
    snd, rcv, gsnd, grcv, stat_snd, stat_rcv, cstat_snd, cstat_rcv, grad_snd, grad_rcv,
    classes, class_grad, class_e, class_pg, class_row,
    e_diag, e_prev, pg_diag, pg_prev, stat_row, cstat_row, acc,
    load_sem, g_send_sem, g_recv_sem, halo_send_sem, halo_recv_sem, relay_sem, back_send_sem, back_recv_sem, back_relay_sem,
    pass_send_sem, send_sem, recv_sem,
):
    s = lax.axis_index("seq")
    hd = lax.axis_index("head")
    others = seq_count - 1
    heads = q_ref.shape[0]
    width = heads * HEAD_DIM
    tiles = STRIDE // TILE
    chunks = seq_count // TILE
    after = lax.rem(s + 1, seq_count)
    part = og_ref.shape[0]

    def head_lanes(h):
        return slice(h * HEAD_DIM, (h + 1) * HEAD_DIM)

    loads = [pltpu.make_async_copy(og_hbm, og_ref, load_sem.at[0])]
    for h in range(heads):
        for j, (src, dst) in enumerate(
            ((q_hbm, q_ref.at[h]), (k_hbm, kv_ref.at[h, 0]), (v_hbm, kv_ref.at[h, 1]))
        ):
            loads.append(
                pltpu.make_async_copy(src.at[:, head_lanes(h)], dst, load_sem.at[1 + 3 * h + j])
            )
    for load in loads:
        load.start()

    barrier = pltpu.get_barrier_semaphore()

    @pl.loop(1, seq_count)
    def _(i):
        pl.semaphore_signal(
            barrier, inc=1, device_id=(lax.rem(s + i, seq_count), hd), device_id_type=MESH
        )

    @pl.loop(1, head_count)
    def _(i):
        pl.semaphore_signal(
            barrier, inc=1, device_id=(s, lax.rem(hd + i, head_count)), device_id_type=MESH
        )

    for load in loads:
        load.wait()
    for h in range(heads):
        for j, ref in enumerate((q_ref.at[h], kv_ref.at[h, 0], kv_ref.at[h, 1])):
            snd[h * tiles : (h + 1) * tiles, j] = ref[...].reshape(tiles, TILE, HEAD_DIM)
    rcv[s] = snd[s]
    own_rows = pl.ds(pl.multiple_of(hd * part, part), part)
    g_home[own_rows, :] = og_ref[:, pl.ds(pl.multiple_of(hd * width, width), width)]

    pl.semaphore_wait(barrier, others + head_count - 1)

    def send(src, dst, index, i):
        peer = lax.rem(s + i, seq_count)
        pltpu.make_async_remote_copy(
            src_ref=src.at[peer],
            dst_ref=dst.at[s],
            send_sem=send_sem.at[index],
            recv_sem=recv_sem.at[index],
            device_id=(peer, hd),
            device_id_type=MESH,
        ).start()

    def whole(src, dst, index):
        return pltpu.make_async_remote_copy(
            src_ref=src.at[pl.ds(0, others)],
            dst_ref=dst.at[pl.ds(0, others)],
            send_sem=send_sem.at[index],
            recv_sem=recv_sem.at[index],
            device_id=(after, hd),
            device_id_type=MESH,
        )

    odd = lax.rem(s, 2) == 1
    even = lax.rem(s, 2) == 0
    direct = heads // 2

    def hop(src, dst, at, send, recv, distance):
        return pltpu.make_async_remote_copy(
            src_ref=src.at[at],
            dst_ref=dst.at[at],
            send_sem=send,
            recv_sem=recv,
            device_id=(lax.rem(s + distance + seq_count, seq_count), hd),
            device_id_type=MESH,
        )

    def hop_relay(src, dst, at, send, recv, distance, to_relay):
        there = (at[0] - direct, at[1])
        return pltpu.make_async_remote_copy(
            src_ref=src.at[at] if to_relay else src.at[there],
            dst_ref=dst.at[there] if to_relay else dst.at[at],
            send_sem=send,
            recv_sem=recv,
            device_id=(lax.rem(s + distance + seq_count, seq_count), hd),
            device_id_type=MESH,
        )

    def halo_hop(at):
        straight = hop(kv_ref, halo, at, halo_send_sem, halo_recv_sem, 1)
        if at[0] < direct:
            straight.start()
            return

        @pl.when(even)
        def _():
            straight.start()

        @pl.when(odd)
        def _():
            halo_to_relay(at).start()

    def halo_to_relay(at):
        sem = relay_sem.at[at[0] - direct, at[1]]
        return hop_relay(kv_ref, relay, at, halo_send_sem, sem, -1, True)

    def halo_pass(at):
        @pl.when(even)
        def _():
            halo_to_relay(at).wait_recv()
            hop_relay(relay, halo, at, pass_send_sem.at[0], halo_recv_sem, 2, False).start()

    def back_hop(at):
        straight = hop(back_snd, back_rcv, at, back_send_sem, back_recv_sem, -1)
        if at[0] < direct:
            straight.start()
            return

        @pl.when(odd)
        def _():
            straight.start()

        @pl.when(even)
        def _():
            back_to_relay(at).start()

    def back_to_relay(at):
        sem = back_relay_sem.at[at[0] - direct, at[1]]
        return hop_relay(back_snd, back_relay, at, back_send_sem, sem, 1, True)

    def back_pass(at):
        @pl.when(odd)
        def _():
            back_to_relay(at).wait_recv()
            hop_relay(back_relay, back_rcv, at, pass_send_sem.at[1], back_recv_sem, -2, False).start()

    def hop_all(src, dst, send, recv):
        return pltpu.make_async_remote_copy(
            src_ref=src, dst_ref=dst, send_sem=send, recv_sem=recv,
            device_id=(after, hd), device_id_type=MESH,
        )

    passed = [(h, j) for h in range(direct, heads) for j in range(2)]
    kept = [(h, j) for h in range(direct) for j in range(2)]
    halo_all = hop_all(kv_ref, halo, halo_send_sem, halo_recv_sem)
    back_all = hop_all(back_snd, back_rcv, back_send_sem, back_recv_sem)

    g_copies = []
    for i in range(1, head_count):
        peer = lax.rem(hd + i, head_count)
        copy = pltpu.make_async_remote_copy(
            src_ref=og_ref.at[:, pl.ds(pl.multiple_of(peer * width, width), width)],
            dst_ref=g_home.at[own_rows, :],
            send_sem=g_send_sem.at[i],
            recv_sem=g_recv_sem.at[i],
            device_id=(s, peer),
            device_id_type=MESH,
        )
        copy.start()
        g_copies.append(copy)

    blocks = passed + kept
    share = seq_count // len(blocks)
    for n, at in enumerate(blocks):
        halo_hop(at)

        @pl.loop(max(1, n * share), (n + 1) * share)
        def _(i):
            send(snd, rcv, 0, i)

        if n >= LAG and n - LAG < len(passed):
            halo_pass(blocks[n - LAG])
    for copy in g_copies:
        copy.wait_recv()
    for h in range(heads):
        gsnd[h * tiles : (h + 1) * tiles] = g_home[
            :, h * HEAD_DIM : (h + 1) * HEAD_DIM
        ].reshape(tiles, TILE, HEAD_DIM)

    @pl.loop(1, seq_count)
    def _(i):
        send(gsnd, grcv, 1, i)

    grcv[s] = gsnd[s]

    halo_all.wait_recv()

    row = iota((STRIDE, STRIDE), 0)
    col = iota((STRIDE, STRIDE), 1)

    def lanes_of(h):
        return pl.ds(pl.multiple_of(h * HEAD_DIM, HEAD_DIM), HEAD_DIM)

    @pl.loop(0, heads)
    def _(h):
        qh, gh = q_ref[h], g_home[:, lanes_of(h)]
        sd = jnp.where(row <= col, dot_nt(kv_ref[h, 0], qh) * SCALE, NEG_LARGE)
        sp = jnp.where((row > col) & (s > 0), dot_nt(halo[h, 0], qh) * SCALE, NEG_LARGE)
        top = jnp.maximum(
            jnp.max(sd, axis=0, keepdims=True), jnp.max(sp, axis=0, keepdims=True)
        )
        ed, ep = jnp.exp(sd - top), jnp.exp(sp - top)
        gd, gp = dot_nt(kv_ref[h, 1], gh), dot_nt(halo[h, 1], gh)
        e_diag[h], e_prev[h], pg_diag[h], pg_prev[h] = ed, ep, gd, gp
        total = jnp.sum(ed + ep, axis=0, keepdims=True)
        weighted = jnp.sum(ed * gd + ep * gp, axis=0, keepdims=True)
        for n, value in enumerate((top, total, weighted)):
            stat_row[n, pl.ds(h, 1), :] = value

    owner = lax.rem(iota((seq_count, STRIDE), 0), tiles) == iota((seq_count, STRIDE), 1) // TILE
    code_row = lax.rem(iota((STRIDE, HEAD_DIM), 0), TILE)
    code_row = lax.rem(code_row, 2) * HALF + code_row // 2
    pick_lane = iota((STRIDE, HEAD_DIM), 1)
    code_col = lax.rem(iota((HEAD_DIM, STRIDE), 1), TILE)
    code_col = lax.rem(code_col, 2) * HALF + code_col // 2
    pick_row = iota((HEAD_DIM, STRIDE), 0)

    coded = jnp.zeros((seq_count, HEAD_DIM), F32)
    for n in range(3):
        values = jnp.broadcast_to(
            stat_row[n][:, None, :], (heads, tiles, STRIDE)
        ).reshape(seq_count, STRIDE)
        select = (pick_lane == code_row + n * PAIRS).astype(F32)
        coded = coded + dot_exact(jnp.where(owner, values, 0.0), select)
    stat_snd[:, 0, :] = coded
    stat_rcv[s] = stat_snd[s]

    @pl.loop(1, seq_count)
    def _(i):
        send(stat_snd, stat_rcv, 2, i)

    swap_row = iota((STRIDE, STRIDE), 0)
    swap_col = iota((STRIDE, STRIDE), 1)
    swap = (
        (swap_row // TILE == lax.rem(swap_col, TILE))
        & (lax.rem(swap_row, TILE) == swap_col // TILE)
    ).astype(BF16)

    whole(snd, rcv, 0).wait_recv()

    def sort_classes(blocks, first):
        for c in range(chunks):
            these = slice(c * TILE, (c + 1) * TILE)
            mixed = jnp.concatenate(
                [block(these).reshape(STRIDE, HEAD_DIM) for block in blocks], axis=1
            )
            sorted_rows = dot_nn(swap, mixed).astype(BF16)
            for j in range(len(blocks)):
                classes[first + j, :, these, :] = sorted_rows[
                    :, j * HEAD_DIM : (j + 1) * HEAD_DIM
                ].reshape(TILE, TILE, HEAD_DIM)

    sort_classes([lambda these, j=j: rcv[these, j] for j in range(3)], 0)

    pair = 2 * seq_count
    prow = iota((pair, pair), 0)
    pcol = iota((pair, pair), 1)
    allowed = ((prow < seq_count) == (pcol < seq_count)) & (prow < pcol)

    def pair_of(j, p):
        return classes[j, 2 * p : 2 * p + 2].reshape(pair, HEAD_DIM)

    class_row[...] = jnp.zeros_like(class_row)
    for p in range(PAIRS):
        sc = jnp.where(allowed, dot_nt(pair_of(1, p), pair_of(0, p)) * SCALE, NEG_LARGE)
        top = jnp.max(sc, axis=0, keepdims=True)
        ec = jnp.where(allowed, jnp.exp(sc - top), 0.0)
        class_e[p] = ec
        class_row[p : p + 1, :] = top
        class_row[PAIRS + p : PAIRS + p + 1, :] = jnp.sum(ec, axis=0, keepdims=True)

    whole(gsnd, grcv, 1).wait_recv()
    sort_classes([lambda these: grcv[these]], 3)
    for p in range(PAIRS):
        pg = dot_nt(pair_of(2, p), pair_of(3, p))
        class_pg[p] = pg
        class_row[2 * PAIRS + p : 2 * PAIRS + p + 1, :] = jnp.sum(
            class_e[p] * pg, axis=0, keepdims=True
        )
    columns = class_row[...].T
    small = iota((seq_count, HEAD_DIM), 1) < HALF
    cstat_snd[:, 0, :] = jnp.where(
        small, columns[:seq_count], pltpu.roll(columns[seq_count:], HALF, 1)
    )
    cstat_rcv[s] = cstat_snd[s]

    @pl.loop(1, seq_count)
    def _(i):
        send(cstat_snd, cstat_rcv, 3, i)

    whole(stat_snd, stat_rcv, 2).wait_recv()
    band = stat_rcv[:, 0, :]
    band_row = jnp.concatenate([band, pltpu.roll(band, HEAD_DIM - HALF, 1)], axis=0).T
    for p in range(PAIRS):
        factor, delta = combine(
            *(class_row[n * PAIRS + p : n * PAIRS + p + 1, :] for n in range(3)),
            *(band_row[n * PAIRS + p : n * PAIRS + p + 1, :] for n in range(3)),
        )
        probs = class_e[p] * factor
        sgrad = (probs * (class_pg[p] - delta)).astype(BF16)
        for j, value in enumerate(
            (
                dot_tn(sgrad, pair_of(1, p)) * SCALE,
                dot_nn(sgrad, pair_of(0, p)) * SCALE,
                dot_nn(probs.astype(BF16), pair_of(3, p)),
            )
        ):
            class_grad[j, 2 * p : 2 * p + 2] = value.astype(BF16).reshape(
                2, seq_count, HEAD_DIM
            )
    for c in range(chunks):
        these = slice(c * TILE, (c + 1) * TILE)
        mixed = jnp.concatenate(
            [class_grad[j, :, these, :].reshape(STRIDE, HEAD_DIM) for j in range(3)], axis=1
        )
        sorted_rows = dot_nn(swap, mixed).astype(BF16)
        for j in range(3):
            grad_snd[these, j] = sorted_rows[:, j * HEAD_DIM : (j + 1) * HEAD_DIM].reshape(
                TILE, TILE, HEAD_DIM
            )
    grad_rcv[s] = grad_snd[s]

    @pl.loop(1, EARLY)
    def _(i):
        send(grad_snd, grad_rcv, 4, i)

    whole(cstat_snd, cstat_rcv, 3).wait_recv()
    got = cstat_rcv[:, 0, :]
    for n in range(3):
        select = (pick_row == code_col + n * PAIRS).astype(F32)
        cstat_row[n] = jnp.sum(
            jnp.where(owner, dot_exact(got, select), 0.0).reshape(heads, tiles, STRIDE), axis=1
        )

    def band_prev(h):
        factor, delta = combine(
            *(stat_row[n, h : h + 1, :] for n in range(3)),
            *(cstat_row[n, h : h + 1, :] for n in range(3)),
        )
        stat_row[0, h : h + 1, :] = factor
        stat_row[1, h : h + 1, :] = delta
        probs = e_prev[h] * factor
        sgrad = (probs * (pg_prev[h] - delta)).astype(BF16)
        back_snd[h, 0] = (dot_nn(sgrad, q_ref[h]) * SCALE).astype(BF16)
        back_snd[h, 1] = dot_nn(probs.astype(BF16), g_home[:, head_lanes(h)]).astype(BF16)
        for j in range(2):
            back_hop((h, j))
        acc[0, h] = dot_tn(sgrad, halo[h, 0])

    def band_own(h):
        factor, delta = (stat_row[n, h : h + 1, :] for n in range(2))
        probs = e_diag[h] * factor
        sgrad = (probs * (pg_diag[h] - delta)).astype(BF16)
        acc[0, h] = (acc[0, h] + dot_tn(sgrad, kv_ref[h, 0])) * SCALE
        acc[1, h] = dot_nn(sgrad, q_ref[h]) * SCALE
        acc[2, h] = dot_nn(probs.astype(BF16), g_home[:, head_lanes(h)])

    for h in range(direct, heads):
        band_prev(h)

    @pl.loop(EARLY, seq_count)
    def _(i):
        send(grad_snd, grad_rcv, 4, i)

    for h in range(direct):
        band_prev(h)
    for h in range(heads):
        band_own(h)
        for at in passed[h * len(passed) // heads : (h + 1) * len(passed) // heads]:
            back_pass(at)

    whole(grad_snd, grad_rcv, 4).wait_recv()
    back_all.wait_recv()
    for h in range(heads):
        for j, out in enumerate((dq_ref, dk_ref, dv_ref)):
            value = acc[j, h] + grad_rcv[h * tiles : (h + 1) * tiles, j].reshape(
                STRIDE, HEAD_DIM
            ).astype(F32)
            if j > 0:
                value = value + back_rcv[h, j - 1].astype(F32)
            out[:, head_lanes(h)] = value.astype(BF16)

    for copy in g_copies:
        copy.wait_send()
    halo_all.wait_send()
    for index, buffers in enumerate(
        ((snd, rcv), (gsnd, grcv), (stat_snd, stat_rcv), (cstat_snd, cstat_rcv), (grad_snd, grad_rcv))
    ):
        whole(*buffers, index).wait_send()
    back_all.wait_send()

    def sent(src, dst, send, recv):
        return hop_all(src, dst.at[pl.ds(0, direct)], send, recv)

    @pl.when(even)
    def _():
        sent(relay, halo, pass_send_sem.at[0], halo_recv_sem).wait_send()

    @pl.when(odd)
    def _():
        sent(back_relay, back_rcv, pass_send_sem.at[1], back_recv_sem).wait_send()


def per_device(queries, keys, values, out_grad):
    length, width = queries.shape
    seq_count = lax.axis_size("seq")
    head_count = lax.axis_size("head")
    heads = width // HEAD_DIM
    assert length == STRIDE and seq_count * TILE == STRIDE * heads and seq_count * 2 == HEAD_DIM
    vmem = pl.BlockSpec(memory_space=pltpu.VMEM)
    far = pl.BlockSpec(memory_space=pltpu.HBM)
    tile = (TILE, HEAD_DIM)
    pair = 2 * seq_count
    grads = pl.pallas_call(
        functools.partial(kernel, seq_count, head_count),
        out_shape=[pltpu.VMEM(queries.shape, BF16)] * 3,
        in_specs=[far] * 4,
        out_specs=[vmem] * 3,
        scratch_shapes=[
            pltpu.VMEM((heads, length, HEAD_DIM), BF16),
            pltpu.VMEM((heads, 2, length, HEAD_DIM), BF16),
            pltpu.VMEM(out_grad.shape, BF16),
            pltpu.VMEM((length, width), BF16),
            pltpu.VMEM((heads, 2, length, HEAD_DIM), BF16),
            pltpu.VMEM((heads // 2, 2, length, HEAD_DIM), BF16),
            pltpu.VMEM((heads, 2, length, HEAD_DIM), BF16),
            pltpu.VMEM((heads, 2, length, HEAD_DIM), BF16),
            pltpu.VMEM((heads // 2, 2, length, HEAD_DIM), BF16),
            pltpu.VMEM((seq_count, 3) + tile, BF16),
            pltpu.VMEM((seq_count, 3) + tile, BF16),
            pltpu.VMEM((seq_count,) + tile, BF16),
            pltpu.VMEM((seq_count,) + tile, BF16),
            pltpu.VMEM((seq_count, 1, HEAD_DIM), F32),
            pltpu.VMEM((seq_count, 1, HEAD_DIM), F32),
            pltpu.VMEM((seq_count, 1, HEAD_DIM), F32),
            pltpu.VMEM((seq_count, 1, HEAD_DIM), F32),
            pltpu.VMEM((seq_count, 3) + tile, BF16),
            pltpu.VMEM((seq_count, 3) + tile, BF16),
            pltpu.VMEM((4, TILE, seq_count, HEAD_DIM), BF16),
            pltpu.VMEM((3, TILE, seq_count, HEAD_DIM), BF16),
            pltpu.VMEM((PAIRS, pair, pair), F32),
            pltpu.VMEM((PAIRS, pair, pair), F32),
            pltpu.VMEM((HEAD_DIM, HEAD_DIM), F32),
            pltpu.VMEM((heads, STRIDE, STRIDE), F32),
            pltpu.VMEM((heads, STRIDE, STRIDE), F32),
            pltpu.VMEM((heads, STRIDE, STRIDE), F32),
            pltpu.VMEM((heads, STRIDE, STRIDE), F32),
            pltpu.VMEM((3, heads, STRIDE), F32),
            pltpu.VMEM((3, heads, STRIDE), F32),
            pltpu.VMEM((3, heads, length, HEAD_DIM), F32),
            pltpu.SemaphoreType.DMA((1 + 3 * heads,)),
            pltpu.SemaphoreType.DMA((head_count,)),
            pltpu.SemaphoreType.DMA((head_count,)),
            pltpu.SemaphoreType.DMA,
            pltpu.SemaphoreType.DMA,
            pltpu.SemaphoreType.DMA((heads // 2, 2)),
            pltpu.SemaphoreType.DMA,
            pltpu.SemaphoreType.DMA,
            pltpu.SemaphoreType.DMA((heads // 2, 2)),
            pltpu.SemaphoreType.DMA((2,)),
            pltpu.SemaphoreType.DMA((5,)),
            pltpu.SemaphoreType.DMA((5,)),
        ],
        compiler_params=pltpu.CompilerParams(
            collective_id=0, has_side_effects=True, vmem_limit_bytes=62 * 2**20
        ),
    )(queries, keys, values, out_grad)
    return grads


def solution(mesh):
    return jax.shard_map(
        per_device,
        mesh=mesh,
        in_specs=(P("seq", "head"), P("seq", "head"), P("seq", "head"), P(("seq", "head"), None)),
        out_specs=(P("seq", "head"), P("seq", "head"), P("seq", "head")),
        check_vma=False,
    )
```

```python
import functools

import jax
import jax.numpy as jnp
from jax import lax
from jax.experimental import pallas as pl
from jax.experimental.pallas import tpu as pltpu
from jax.sharding import PartitionSpec as P

HEAD_DIM = 128
STRIDE = 256
TILE = 16
PAIRS = TILE // 2
HALF = 32
NEG_LARGE = -1e30
SCALE = HEAD_DIM**-0.5
EARLY = 37
UNROLL = 9
MESH = pl.DeviceIdType.MESH
F32 = jnp.float32
BF16 = jnp.bfloat16


def dot_nt(a, b):
    return lax.dot_general(a, b, (((1,), (1,)), ((), ())), preferred_element_type=F32)


def dot_nn(a, b):
    return lax.dot_general(a, b, (((1,), (0,)), ((), ())), preferred_element_type=F32)


def dot_tn(a, b):
    return lax.dot_general(a, b, (((0,), (0,)), ((), ())), preferred_element_type=F32)


def dot_exact(a, b):
    return lax.dot_general(
        a, b, (((1,), (0,)), ((), ())),
        preferred_element_type=F32, precision=lax.Precision.HIGHEST,
    )


def iota(shape, axis):
    return lax.broadcasted_iota(jnp.int32, shape, axis)


def combine(top, total, weighted, other_top, other_total, other_weighted):
    peak = jnp.maximum(top, other_top)
    mine, theirs = jnp.exp(top - peak), jnp.exp(other_top - peak)
    inverse = 1.0 / (total * mine + other_total * theirs)
    return mine * inverse, (weighted * mine + other_weighted * theirs) * inverse


def kernel(
    seq_count, head_count,
    q_hbm, k_hbm, v_hbm, og_hbm,
    out_ref,
    q_ref, kv_ref, og_ref, g_home, halo, relay, back_snd, back_rcv, back_relay,
    snd, rcv, gsnd, grcv, stat_snd, stat_rcv, cstat_snd, cstat_rcv, grad_snd, grad_rcv,
    classes, class_grad, class_e, class_pg, class_row,
    e_diag, e_prev, pg_diag, pg_prev, part_row, stat_row, cstat_row, acc,
    load_sem, g_send_sem, g_recv_sem, halo_send_sem, halo_recv_sem, relay_sem, back_send_sem, back_recv_sem, back_relay_sem,
    pass_send_sem, send_sem, recv_sem,
):
    s = lax.axis_index("seq")
    hd = lax.axis_index("head")
    others = seq_count - 1
    heads = q_ref.shape[0]
    width = heads * HEAD_DIM
    tiles = STRIDE // TILE
    chunks = seq_count // TILE
    after = lax.rem(s + 1, seq_count)
    part = og_ref.shape[0]

    def head_lanes(h):
        return slice(h * HEAD_DIM, (h + 1) * HEAD_DIM)

    loads = [pltpu.make_async_copy(og_hbm, og_ref, load_sem.at[0])]
    for h in range(heads):
        for j, (src, dst) in enumerate(
            ((q_hbm, q_ref.at[h]), (k_hbm, kv_ref.at[h, 0]), (v_hbm, kv_ref.at[h, 1]))
        ):
            loads.append(
                pltpu.make_async_copy(src.at[:, head_lanes(h)], dst, load_sem.at[1 + 3 * h + j])
            )
    for load in loads:
        load.start()

    barrier = pltpu.get_barrier_semaphore()

    @pl.loop(1, seq_count, unroll=UNROLL)
    def _(i):
        pl.semaphore_signal(
            barrier, inc=1, device_id=(lax.rem(s + i, seq_count), hd), device_id_type=MESH
        )

    @pl.loop(1, head_count)
    def _(i):
        pl.semaphore_signal(
            barrier, inc=1, device_id=(s, lax.rem(hd + i, head_count)), device_id_type=MESH
        )

    for load in loads:
        load.wait()
    for h in range(heads):
        for j, ref in enumerate((q_ref.at[h], kv_ref.at[h, 0], kv_ref.at[h, 1])):
            snd[h * tiles : (h + 1) * tiles, j] = ref[...].reshape(tiles, TILE, HEAD_DIM)
    rcv[s] = snd[s]
    own_rows = pl.ds(pl.multiple_of(hd * part, part), part)
    g_home[own_rows, :] = og_ref[:, pl.ds(pl.multiple_of(hd * width, width), width)]

    pl.semaphore_wait(barrier, others + head_count - 1)

    def send(src, dst, index, i):
        peer = lax.rem(s + i, seq_count)
        pltpu.make_async_remote_copy(
            src_ref=src.at[peer],
            dst_ref=dst.at[s],
            send_sem=send_sem.at[index],
            recv_sem=recv_sem.at[index],
            device_id=(peer, hd),
            device_id_type=MESH,
        ).start()

    def whole(src, dst, index):
        return pltpu.make_async_remote_copy(
            src_ref=src.at[pl.ds(0, others)],
            dst_ref=dst.at[pl.ds(0, others)],
            send_sem=send_sem.at[index],
            recv_sem=recv_sem.at[index],
            device_id=(after, hd),
            device_id_type=MESH,
        )

    odd = lax.rem(s, 2) == 1
    even = lax.rem(s, 2) == 0
    direct = heads // 2

    def hop(src, dst, at, send, recv, distance):
        return pltpu.make_async_remote_copy(
            src_ref=src.at[at],
            dst_ref=dst.at[at],
            send_sem=send,
            recv_sem=recv,
            device_id=(lax.rem(s + distance + seq_count, seq_count), hd),
            device_id_type=MESH,
        )

    def hop_relay(src, dst, at, send, recv, distance, to_relay):
        there = (at[0] - direct, at[1])
        return pltpu.make_async_remote_copy(
            src_ref=src.at[at] if to_relay else src.at[there],
            dst_ref=dst.at[there] if to_relay else dst.at[at],
            send_sem=send,
            recv_sem=recv,
            device_id=(lax.rem(s + distance + seq_count, seq_count), hd),
            device_id_type=MESH,
        )

    def halo_hop(at):
        straight = hop(kv_ref, halo, at, halo_send_sem, halo_recv_sem, 1)
        if at[0] < direct:
            straight.start()
            return

        @pl.when(even)
        def _():
            straight.start()

        @pl.when(odd)
        def _():
            halo_to_relay(at).start()

    def halo_to_relay(at):
        sem = relay_sem.at[at[0] - direct, at[1]]
        return hop_relay(kv_ref, relay, at, halo_send_sem, sem, -1, True)

    def halo_pass(at):
        @pl.when(even)
        def _():
            halo_to_relay(at).wait_recv()
            hop_relay(relay, halo, at, pass_send_sem.at[0], halo_recv_sem, 2, False).start()

    def back_hop(at):
        straight = hop(back_snd, back_rcv, at, back_send_sem, back_recv_sem, -1)
        if at[0] < direct:
            straight.start()
            return

        @pl.when(odd)
        def _():
            straight.start()

        @pl.when(even)
        def _():
            back_to_relay(at).start()

    def back_to_relay(at):
        sem = back_relay_sem.at[at[0] - direct, at[1]]
        return hop_relay(back_snd, back_relay, at, back_send_sem, sem, 1, True)

    def back_pass(at):
        @pl.when(odd)
        def _():
            back_to_relay(at).wait_recv()
            hop_relay(back_relay, back_rcv, at, pass_send_sem.at[1], back_recv_sem, -2, False).start()

    def hop_all(src, dst, send, recv):
        return pltpu.make_async_remote_copy(
            src_ref=src, dst_ref=dst, send_sem=send, recv_sem=recv,
            device_id=(after, hd), device_id_type=MESH,
        )

    passed = [(h, j) for h in range(direct, heads) for j in range(2)]
    kept = [(h, j) for h in range(direct) for j in range(2)]
    halo_all = hop_all(kv_ref, halo, halo_send_sem, halo_recv_sem)
    back_all = hop_all(back_snd, back_rcv, back_send_sem, back_recv_sem)

    g_copies = []
    for i in range(1, head_count):
        peer = lax.rem(hd + i, head_count)
        copy = pltpu.make_async_remote_copy(
            src_ref=og_ref.at[:, pl.ds(pl.multiple_of(peer * width, width), width)],
            dst_ref=g_home.at[own_rows, :],
            send_sem=g_send_sem.at[i],
            recv_sem=g_recv_sem.at[i],
            device_id=(s, peer),
            device_id_type=MESH,
        )
        copy.start()
        g_copies.append(copy)

    blocks = passed + kept
    share = seq_count // len(blocks)
    for n, at in enumerate(blocks):
        halo_hop(at)

        @pl.loop(max(1, n * share), (n + 1) * share, unroll=True)
        def _(i):
            send(snd, rcv, 0, i)

    for copy in g_copies:
        copy.wait_recv()
    for h in range(heads):
        gsnd[h * tiles : (h + 1) * tiles] = g_home[
            :, h * HEAD_DIM : (h + 1) * HEAD_DIM
        ].reshape(tiles, TILE, HEAD_DIM)

    @pl.loop(1, seq_count, unroll=UNROLL)
    def _(i):
        send(gsnd, grcv, 1, i)

    grcv[s] = gsnd[s]

    row = iota((STRIDE, STRIDE), 0)
    col = iota((STRIDE, STRIDE), 1)

    def band_part(h, keys, values, mask, e_part, pg_part, part):
        sc = jnp.where(mask, dot_nt(keys, q_ref[h]) * SCALE, NEG_LARGE)
        top = jnp.max(sc, axis=0, keepdims=True)
        ex = jnp.exp(sc - top)
        pg = dot_nt(values, g_home[:, head_lanes(h)])
        e_part[h], pg_part[h] = ex, pg
        total = jnp.sum(ex, axis=0, keepdims=True)
        weighted = jnp.sum(ex * pg, axis=0, keepdims=True)
        for n, value in enumerate((top, total, weighted)):
            part_row[part, n, h : h + 1, :] = value

    for h in range(heads):
        band_part(h, kv_ref[h, 0], kv_ref[h, 1], row <= col, e_diag, pg_diag, 0)
    for at in passed:
        halo_pass(at)

    swap_row = iota((STRIDE, STRIDE), 0)
    swap_col = iota((STRIDE, STRIDE), 1)
    swap = (
        (swap_row // TILE == lax.rem(swap_col, TILE))
        & (lax.rem(swap_row, TILE) == swap_col // TILE)
    ).astype(BF16)

    whole(snd, rcv, 0).wait_recv()

    def sort_classes(blocks, first):
        for c in range(chunks):
            these = slice(c * TILE, (c + 1) * TILE)
            mixed = jnp.concatenate(
                [block(these).reshape(STRIDE, HEAD_DIM) for block in blocks], axis=1
            )
            sorted_rows = dot_nn(swap, mixed).astype(BF16)
            for j in range(len(blocks)):
                classes[first + j, :, these, :] = sorted_rows[
                    :, j * HEAD_DIM : (j + 1) * HEAD_DIM
                ].reshape(TILE, TILE, HEAD_DIM)

    sort_classes([lambda these, j=j: rcv[these, j] for j in range(3)], 0)

    pair = 2 * seq_count
    prow = iota((pair, pair), 0)
    pcol = iota((pair, pair), 1)
    allowed = ((prow < seq_count) == (pcol < seq_count)) & (prow < pcol)

    def pair_of(j, p):
        return classes[j, 2 * p : 2 * p + 2].reshape(pair, HEAD_DIM)

    class_row[...] = jnp.zeros_like(class_row)
    for p in range(PAIRS):
        sc = jnp.where(allowed, dot_nt(pair_of(1, p), pair_of(0, p)) * SCALE, NEG_LARGE)
        top = jnp.max(sc, axis=0, keepdims=True)
        ec = jnp.where(allowed, jnp.exp(sc - top), 0.0)
        class_e[p] = ec
        class_row[p : p + 1, :] = top
        class_row[PAIRS + p : PAIRS + p + 1, :] = jnp.sum(ec, axis=0, keepdims=True)

    halo_all.wait_recv()
    for h in range(heads):
        band_part(h, halo[h, 0], halo[h, 1], (row > col) & (s > 0), e_prev, pg_prev, 1)
    tops = [part_row[part, 0] for part in range(2)]
    stat_row[0] = jnp.maximum(*tops)
    stat_row[1] = jnp.zeros_like(tops[0])
    stat_row[2] = jnp.zeros_like(tops[0])
    for part in range(2):
        level = jnp.exp(tops[part] - stat_row[0])
        for n in range(1, 3):
            stat_row[n] += part_row[part, n] * level
        part_row[part, 0] = level

    owner = lax.rem(iota((seq_count, STRIDE), 0), tiles) == iota((seq_count, STRIDE), 1) // TILE
    code_row = lax.rem(iota((STRIDE, HEAD_DIM), 0), TILE)
    code_row = lax.rem(code_row, 2) * HALF + code_row // 2
    pick_lane = iota((STRIDE, HEAD_DIM), 1)
    code_col = lax.rem(iota((HEAD_DIM, STRIDE), 1), TILE)
    code_col = lax.rem(code_col, 2) * HALF + code_col // 2
    pick_row = iota((HEAD_DIM, STRIDE), 0)

    coded = jnp.zeros((seq_count, HEAD_DIM), F32)
    for n in range(3):
        values = jnp.broadcast_to(
            stat_row[n][:, None, :], (heads, tiles, STRIDE)
        ).reshape(seq_count, STRIDE)
        select = (pick_lane == code_row + n * PAIRS).astype(F32)
        coded = coded + dot_exact(jnp.where(owner, values, 0.0), select)
    stat_snd[:, 0, :] = coded
    stat_rcv[s] = stat_snd[s]

    @pl.loop(1, seq_count, unroll=UNROLL)
    def _(i):
        send(stat_snd, stat_rcv, 2, i)

    whole(gsnd, grcv, 1).wait_recv()
    sort_classes([lambda these: grcv[these]], 3)
    for p in range(PAIRS):
        pg = dot_nt(pair_of(2, p), pair_of(3, p))
        class_pg[p] = pg
        class_row[2 * PAIRS + p : 2 * PAIRS + p + 1, :] = jnp.sum(
            class_e[p] * pg, axis=0, keepdims=True
        )
    columns = class_row[...].T
    small = iota((seq_count, HEAD_DIM), 1) < HALF
    cstat_snd[:, 0, :] = jnp.where(
        small, columns[:seq_count], pltpu.roll(columns[seq_count:], HALF, 1)
    )
    cstat_rcv[s] = cstat_snd[s]

    @pl.loop(1, seq_count, unroll=UNROLL)
    def _(i):
        send(cstat_snd, cstat_rcv, 3, i)

    whole(stat_snd, stat_rcv, 2).wait_recv()
    band = stat_rcv[:, 0, :]
    band_row = jnp.concatenate([band, pltpu.roll(band, HEAD_DIM - HALF, 1)], axis=0).T
    for p in range(PAIRS):
        factor, delta = combine(
            *(class_row[n * PAIRS + p : n * PAIRS + p + 1, :] for n in range(3)),
            *(band_row[n * PAIRS + p : n * PAIRS + p + 1, :] for n in range(3)),
        )
        probs = class_e[p] * factor
        sgrad = (probs * (class_pg[p] - delta)).astype(BF16)
        for j, value in enumerate(
            (
                dot_tn(sgrad, pair_of(1, p)) * SCALE,
                dot_nn(sgrad, pair_of(0, p)) * SCALE,
                dot_nn(probs.astype(BF16), pair_of(3, p)),
            )
        ):
            class_grad[j, 2 * p : 2 * p + 2] = value.astype(BF16).reshape(
                2, seq_count, HEAD_DIM
            )
    for c in range(chunks):
        these = slice(c * TILE, (c + 1) * TILE)
        mixed = jnp.concatenate(
            [class_grad[j, :, these, :].reshape(STRIDE, HEAD_DIM) for j in range(3)], axis=1
        )
        sorted_rows = dot_nn(swap, mixed).astype(BF16)
        for j in range(3):
            grad_snd[these, j] = sorted_rows[:, j * HEAD_DIM : (j + 1) * HEAD_DIM].reshape(
                TILE, TILE, HEAD_DIM
            )
    grad_rcv[s] = grad_snd[s]

    @pl.loop(1, EARLY, unroll=UNROLL)
    def _(i):
        send(grad_snd, grad_rcv, 4, i)

    whole(cstat_snd, cstat_rcv, 3).wait_recv()
    got = cstat_rcv[:, 0, :]
    for n in range(3):
        select = (pick_row == code_col + n * PAIRS).astype(F32)
        cstat_row[n] = jnp.sum(
            jnp.where(owner, dot_exact(got, select), 0.0).reshape(heads, tiles, STRIDE), axis=1
        )

    def band_prev(h):
        factor, delta = combine(
            *(stat_row[n, h : h + 1, :] for n in range(3)),
            *(cstat_row[n, h : h + 1, :] for n in range(3)),
        )
        stat_row[0, h : h + 1, :] = factor
        stat_row[1, h : h + 1, :] = delta
        probs = e_prev[h] * (factor * part_row[1, 0, h : h + 1, :])
        sgrad = (probs * (pg_prev[h] - delta)).astype(BF16)
        back_snd[h, 0] = (dot_nn(sgrad, q_ref[h]) * SCALE).astype(BF16)
        back_snd[h, 1] = dot_nn(probs.astype(BF16), g_home[:, head_lanes(h)]).astype(BF16)
        for j in range(2):
            back_hop((h, j))
        acc[0, h] = dot_tn(sgrad, halo[h, 0])

    def band_own(h):
        factor, delta = (stat_row[n, h : h + 1, :] for n in range(2))
        probs = e_diag[h] * (factor * part_row[0, 0, h : h + 1, :])
        sgrad = (probs * (pg_diag[h] - delta)).astype(BF16)
        acc[0, h] = (acc[0, h] + dot_tn(sgrad, kv_ref[h, 0])) * SCALE
        acc[1, h] = dot_nn(sgrad, q_ref[h]) * SCALE
        acc[2, h] = dot_nn(probs.astype(BF16), g_home[:, head_lanes(h)])

    for h in range(direct, heads):
        band_prev(h)

    @pl.loop(EARLY, seq_count, unroll=UNROLL)
    def _(i):
        send(grad_snd, grad_rcv, 4, i)

    for h in range(direct):
        band_prev(h)
    for h in range(heads):
        band_own(h)
        for at in passed[h * len(passed) // heads : (h + 1) * len(passed) // heads]:
            back_pass(at)

    whole(grad_snd, grad_rcv, 4).wait_recv()
    for j in range(3):
        for h in range(heads):
            value = acc[j, h] + grad_rcv[h * tiles : (h + 1) * tiles, j].reshape(
                STRIDE, HEAD_DIM
            ).astype(F32)
            if j == 0:
                out_ref[0, :, head_lanes(h)] = value.astype(BF16)
            else:
                acc[j, h] = value
    back_all.wait_recv()
    for h in range(heads):
        for j in range(2):
            out_ref[1 + j, :, head_lanes(h)] = (acc[1 + j, h] + back_rcv[h, j].astype(F32)).astype(BF16)

    for copy in g_copies:
        copy.wait_send()
    halo_all.wait_send()
    for index, buffers in enumerate(
        ((snd, rcv), (gsnd, grcv), (stat_snd, stat_rcv), (cstat_snd, cstat_rcv), (grad_snd, grad_rcv))
    ):
        whole(*buffers, index).wait_send()
    back_all.wait_send()

    def sent(src, dst, send, recv):
        return hop_all(src, dst.at[pl.ds(0, direct)], send, recv)

    @pl.when(even)
    def _():
        sent(relay, halo, pass_send_sem.at[0], halo_recv_sem).wait_send()

    @pl.when(odd)
    def _():
        sent(back_relay, back_rcv, pass_send_sem.at[1], back_recv_sem).wait_send()


def per_device(queries, keys, values, out_grad):
    length, width = queries.shape
    seq_count = lax.axis_size("seq")
    head_count = lax.axis_size("head")
    heads = width // HEAD_DIM
    assert length == STRIDE and seq_count * TILE == STRIDE * heads and seq_count * 2 == HEAD_DIM
    vmem = pl.BlockSpec(memory_space=pltpu.VMEM)
    far = pl.BlockSpec(memory_space=pltpu.HBM)
    tile = (TILE, HEAD_DIM)
    pair = 2 * seq_count
    grads = pl.pallas_call(
        functools.partial(kernel, seq_count, head_count),
        out_shape=pltpu.VMEM((3,) + queries.shape, BF16),
        in_specs=[far] * 4,
        out_specs=vmem,
        scratch_shapes=[
            pltpu.VMEM((heads, length, HEAD_DIM), BF16),
            pltpu.VMEM((heads, 2, length, HEAD_DIM), BF16),
            pltpu.VMEM(out_grad.shape, BF16),
            pltpu.VMEM((length, width), BF16),
            pltpu.VMEM((heads, 2, length, HEAD_DIM), BF16),
            pltpu.VMEM((heads // 2, 2, length, HEAD_DIM), BF16),
            pltpu.VMEM((heads, 2, length, HEAD_DIM), BF16),
            pltpu.VMEM((heads, 2, length, HEAD_DIM), BF16),
            pltpu.VMEM((heads // 2, 2, length, HEAD_DIM), BF16),
            pltpu.VMEM((seq_count, 3) + tile, BF16),
            pltpu.VMEM((seq_count, 3) + tile, BF16),
            pltpu.VMEM((seq_count,) + tile, BF16),
            pltpu.VMEM((seq_count,) + tile, BF16),
            pltpu.VMEM((seq_count, 1, HEAD_DIM), F32),
            pltpu.VMEM((seq_count, 1, HEAD_DIM), F32),
            pltpu.VMEM((seq_count, 1, HEAD_DIM), F32),
            pltpu.VMEM((seq_count, 1, HEAD_DIM), F32),
            pltpu.VMEM((seq_count, 3) + tile, BF16),
            pltpu.VMEM((seq_count, 3) + tile, BF16),
            pltpu.VMEM((4, TILE, seq_count, HEAD_DIM), BF16),
            pltpu.VMEM((3, TILE, seq_count, HEAD_DIM), BF16),
            pltpu.VMEM((PAIRS, pair, pair), F32),
            pltpu.VMEM((PAIRS, pair, pair), F32),
            pltpu.VMEM((HEAD_DIM, HEAD_DIM), F32),
            pltpu.VMEM((heads, STRIDE, STRIDE), F32),
            pltpu.VMEM((heads, STRIDE, STRIDE), F32),
            pltpu.VMEM((heads, STRIDE, STRIDE), F32),
            pltpu.VMEM((heads, STRIDE, STRIDE), F32),
            pltpu.VMEM((2, 3, heads, STRIDE), F32),
            pltpu.VMEM((3, heads, STRIDE), F32),
            pltpu.VMEM((3, heads, STRIDE), F32),
            pltpu.VMEM((3, heads, length, HEAD_DIM), F32),
            pltpu.SemaphoreType.DMA((1 + 3 * heads,)),
            pltpu.SemaphoreType.DMA((head_count,)),
            pltpu.SemaphoreType.DMA((head_count,)),
            pltpu.SemaphoreType.DMA,
            pltpu.SemaphoreType.DMA,
            pltpu.SemaphoreType.DMA((heads // 2, 2)),
            pltpu.SemaphoreType.DMA,
            pltpu.SemaphoreType.DMA,
            pltpu.SemaphoreType.DMA((heads // 2, 2)),
            pltpu.SemaphoreType.DMA((2,)),
            pltpu.SemaphoreType.DMA((5,)),
            pltpu.SemaphoreType.DMA((5,)),
        ],
        compiler_params=pltpu.CompilerParams(
            collective_id=0, has_side_effects=True, vmem_limit_bytes=62 * 2**20
        ),
    )(queries, keys, values, out_grad)
    return grads[0], grads[1], grads[2]


def solution(mesh):
    return jax.shard_map(
        per_device,
        mesh=mesh,
        in_specs=(P("seq", "head"), P("seq", "head"), P("seq", "head"), P(("seq", "head"), None)),
        out_specs=(P("seq", "head"), P("seq", "head"), P("seq", "head")),
        check_vma=False,
    )
```

```python
import functools

import jax
import jax.numpy as jnp
from jax import lax
from jax.experimental import pallas as pl
from jax.experimental.pallas import tpu as pltpu
from jax.sharding import PartitionSpec as P

HEAD_DIM = 128
STRIDE = 256
TILE = 16
PAIRS = TILE // 2
HALF = 32
NEG_LARGE = -1e30
SCALE = HEAD_DIM**-0.5
EARLY = 37
UNROLL = 9
MESH = pl.DeviceIdType.MESH
F32 = jnp.float32
BF16 = jnp.bfloat16


def dot_nt(a, b):
    return lax.dot_general(a, b, (((1,), (1,)), ((), ())), preferred_element_type=F32)


def dot_nn(a, b):
    return lax.dot_general(a, b, (((1,), (0,)), ((), ())), preferred_element_type=F32)


def dot_tn(a, b):
    return lax.dot_general(a, b, (((0,), (0,)), ((), ())), preferred_element_type=F32)


def dot_exact(a, b):
    return lax.dot_general(
        a, b, (((1,), (0,)), ((), ())),
        preferred_element_type=F32, precision=lax.Precision.HIGHEST,
    )


def iota(shape, axis):
    return lax.broadcasted_iota(jnp.int32, shape, axis)


def combine(top, total, weighted, other_top, other_total, other_weighted):
    peak = jnp.maximum(top, other_top)
    mine, theirs = jnp.exp(top - peak), jnp.exp(other_top - peak)
    inverse = 1.0 / (total * mine + other_total * theirs)
    return mine * inverse, (weighted * mine + other_weighted * theirs) * inverse


def kernel(
    seq_count, head_count,
    q_hbm, k_hbm, v_hbm, og_hbm,
    out_ref,
    q_ref, kv_ref, og_ref, g_home, halo, relay, back_snd, back_rcv, back_relay,
    snd, rcv, gsnd, grcv, stat_snd, stat_rcv, cstat_snd, cstat_rcv, grad_snd, grad_rcv,
    classes, class_grad, class_e, class_pg, class_row,
    e_diag, e_prev, pg_diag, pg_prev, part_row, stat_row, cstat_row, acc,
    load_sem, g_send_sem, g_recv_sem, halo_send_sem, halo_recv_sem, relay_sem, back_send_sem, back_recv_sem, back_relay_sem,
    pass_send_sem, send_sem, recv_sem,
):
    s = lax.axis_index("seq")
    hd = lax.axis_index("head")
    others = seq_count - 1
    heads = q_ref.shape[0]
    width = heads * HEAD_DIM
    tiles = STRIDE // TILE
    chunks = seq_count // TILE
    after = lax.rem(s + 1, seq_count)
    part = og_ref.shape[0]

    def head_lanes(h):
        return slice(h * HEAD_DIM, (h + 1) * HEAD_DIM)

    loads = [pltpu.make_async_copy(og_hbm, og_ref, load_sem.at[0])]
    for h in range(heads):
        for j, (src, dst) in enumerate(
            ((q_hbm, q_ref.at[h]), (k_hbm, kv_ref.at[h, 0]), (v_hbm, kv_ref.at[h, 1]))
        ):
            loads.append(
                pltpu.make_async_copy(src.at[:, head_lanes(h)], dst, load_sem.at[1 + 3 * h + j])
            )
    for load in loads:
        load.start()

    barrier = pltpu.get_barrier_semaphore()

    @pl.loop(1, seq_count, unroll=UNROLL)
    def _(i):
        pl.semaphore_signal(
            barrier, inc=1, device_id=(lax.rem(s + i, seq_count), hd), device_id_type=MESH
        )

    @pl.loop(1, head_count)
    def _(i):
        pl.semaphore_signal(
            barrier, inc=1, device_id=(s, lax.rem(hd + i, head_count)), device_id_type=MESH
        )

    for load in loads:
        load.wait()
    for h in range(heads):
        for j, ref in enumerate((q_ref.at[h], kv_ref.at[h, 0], kv_ref.at[h, 1])):
            snd[h * tiles : (h + 1) * tiles, j] = ref[...].reshape(tiles, TILE, HEAD_DIM)
    rcv[s] = snd[s]
    own_rows = pl.ds(pl.multiple_of(hd * part, part), part)
    g_home[own_rows, :] = og_ref[:, pl.ds(pl.multiple_of(hd * width, width), width)]

    pl.semaphore_wait(barrier, others + head_count - 1)

    def send(src, dst, index, i):
        peer = lax.rem(s + i, seq_count)
        pltpu.make_async_remote_copy(
            src_ref=src.at[peer],
            dst_ref=dst.at[s],
            send_sem=send_sem.at[index],
            recv_sem=recv_sem.at[index],
            device_id=(peer, hd),
            device_id_type=MESH,
        ).start()

    def whole(src, dst, index):
        return pltpu.make_async_remote_copy(
            src_ref=src.at[pl.ds(0, others)],
            dst_ref=dst.at[pl.ds(0, others)],
            send_sem=send_sem.at[index],
            recv_sem=recv_sem.at[index],
            device_id=(after, hd),
            device_id_type=MESH,
        )

    odd = lax.rem(s, 2) == 1
    even = lax.rem(s, 2) == 0
    direct = heads // 2

    def hop(src, dst, at, send, recv, distance):
        return pltpu.make_async_remote_copy(
            src_ref=src.at[at],
            dst_ref=dst.at[at],
            send_sem=send,
            recv_sem=recv,
            device_id=(lax.rem(s + distance + seq_count, seq_count), hd),
            device_id_type=MESH,
        )

    def hop_relay(src, dst, at, send, recv, distance, to_relay):
        there = (at[0] - direct, at[1])
        return pltpu.make_async_remote_copy(
            src_ref=src.at[at] if to_relay else src.at[there],
            dst_ref=dst.at[there] if to_relay else dst.at[at],
            send_sem=send,
            recv_sem=recv,
            device_id=(lax.rem(s + distance + seq_count, seq_count), hd),
            device_id_type=MESH,
        )

    def halo_hop(at):
        straight = hop(kv_ref, halo, at, halo_send_sem, halo_recv_sem, 1)
        if at[0] < direct:
            straight.start()
            return

        @pl.when(even)
        def _():
            straight.start()

        @pl.when(odd)
        def _():
            halo_to_relay(at).start()

    def halo_to_relay(at):
        sem = relay_sem.at[at[0] - direct, at[1]]
        return hop_relay(kv_ref, relay, at, halo_send_sem, sem, -1, True)

    def halo_pass(at):
        @pl.when(even)
        def _():
            halo_to_relay(at).wait_recv()
            hop_relay(relay, halo, at, pass_send_sem.at[0], halo_recv_sem, 2, False).start()

    def back_hop(at):
        straight = hop(back_snd, back_rcv, at, back_send_sem, back_recv_sem, -1)
        if at[0] < direct:
            straight.start()
            return

        @pl.when(odd)
        def _():
            straight.start()

        @pl.when(even)
        def _():
            back_to_relay(at).start()

    def back_to_relay(at):
        sem = back_relay_sem.at[at[0] - direct, at[1]]
        return hop_relay(back_snd, back_relay, at, back_send_sem, sem, 1, True)

    def back_pass(at):
        @pl.when(odd)
        def _():
            back_to_relay(at).wait_recv()
            hop_relay(back_relay, back_rcv, at, pass_send_sem.at[1], back_recv_sem, -2, False).start()

    def hop_all(src, dst, send, recv):
        return pltpu.make_async_remote_copy(
            src_ref=src, dst_ref=dst, send_sem=send, recv_sem=recv,
            device_id=(after, hd), device_id_type=MESH,
        )

    passed = [(h, j) for h in range(direct, heads) for j in range(2)]
    kept = [(h, j) for h in range(direct) for j in range(2)]
    halo_all = hop_all(kv_ref, halo, halo_send_sem, halo_recv_sem)
    back_all = hop_all(back_snd, back_rcv, back_send_sem, back_recv_sem)

    g_copies = []
    for i in range(1, head_count):
        peer = lax.rem(hd + i, head_count)
        copy = pltpu.make_async_remote_copy(
            src_ref=og_ref.at[:, pl.ds(pl.multiple_of(peer * width, width), width)],
            dst_ref=g_home.at[own_rows, :],
            send_sem=g_send_sem.at[i],
            recv_sem=g_recv_sem.at[i],
            device_id=(s, peer),
            device_id_type=MESH,
        )
        copy.start()
        g_copies.append(copy)

    blocks = passed + kept
    share = seq_count // len(blocks)
    for n, at in enumerate(blocks):
        halo_hop(at)

        @pl.loop(max(1, n * share), (n + 1) * share, unroll=True)
        def _(i):
            send(snd, rcv, 0, i)

    for at in passed[:2]:
        halo_pass(at)

    for copy in g_copies:
        copy.wait_recv()
    for h in range(heads):
        gsnd[h * tiles : (h + 1) * tiles] = g_home[
            :, h * HEAD_DIM : (h + 1) * HEAD_DIM
        ].reshape(tiles, TILE, HEAD_DIM)

    @pl.loop(1, seq_count, unroll=UNROLL)
    def _(i):
        send(gsnd, grcv, 1, i)

    grcv[s] = gsnd[s]

    row = iota((STRIDE, STRIDE), 0)
    col = iota((STRIDE, STRIDE), 1)

    def band_part(h, keys, values, mask, e_part, pg_part, part):
        sc = jnp.where(mask, dot_nt(keys, q_ref[h]) * SCALE, NEG_LARGE)
        top = jnp.max(sc, axis=0, keepdims=True)
        ex = jnp.exp(sc - top)
        pg = dot_nt(values, g_home[:, head_lanes(h)])
        e_part[h], pg_part[h] = ex, pg
        total = jnp.sum(ex, axis=0, keepdims=True)
        weighted = jnp.sum(ex * pg, axis=0, keepdims=True)
        for n, value in enumerate((top, total, weighted)):
            part_row[part, n, h : h + 1, :] = value

    for h in range(heads):
        band_part(h, kv_ref[h, 0], kv_ref[h, 1], row <= col, e_diag, pg_diag, 0)
    for at in passed[2:]:
        halo_pass(at)

    swap_row = iota((STRIDE, STRIDE), 0)
    swap_col = iota((STRIDE, STRIDE), 1)
    swap = (
        (swap_row // TILE == lax.rem(swap_col, TILE))
        & (lax.rem(swap_row, TILE) == swap_col // TILE)
    ).astype(BF16)

    whole(snd, rcv, 0).wait_recv()

    def sort_classes(blocks, first):
        for c in range(chunks):
            these = slice(c * TILE, (c + 1) * TILE)
            mixed = jnp.concatenate(
                [block(these).reshape(STRIDE, HEAD_DIM) for block in blocks], axis=1
            )
            sorted_rows = dot_nn(swap, mixed).astype(BF16)
            for j in range(len(blocks)):
                classes[first + j, :, these, :] = sorted_rows[
                    :, j * HEAD_DIM : (j + 1) * HEAD_DIM
                ].reshape(TILE, TILE, HEAD_DIM)

    sort_classes([lambda these, j=j: rcv[these, j] for j in range(3)], 0)

    pair = 2 * seq_count
    prow = iota((pair, pair), 0)
    pcol = iota((pair, pair), 1)
    allowed = ((prow < seq_count) == (pcol < seq_count)) & (prow < pcol)

    def pair_of(j, p):
        return classes[j, 2 * p : 2 * p + 2].reshape(pair, HEAD_DIM)

    class_row[...] = jnp.zeros_like(class_row)
    for p in range(PAIRS):
        sc = jnp.where(allowed, dot_nt(pair_of(1, p), pair_of(0, p)) * SCALE, NEG_LARGE)
        top = jnp.max(sc, axis=0, keepdims=True)
        ec = jnp.where(allowed, jnp.exp(sc - top), 0.0)
        class_e[p] = ec
        class_row[p : p + 1, :] = top
        class_row[PAIRS + p : PAIRS + p + 1, :] = jnp.sum(ec, axis=0, keepdims=True)

    halo_all.wait_recv()
    for h in range(heads):
        band_part(h, halo[h, 0], halo[h, 1], (row > col) & (s > 0), e_prev, pg_prev, 1)
    tops = [part_row[part, 0] for part in range(2)]
    stat_row[0] = jnp.maximum(*tops)
    stat_row[1] = jnp.zeros_like(tops[0])
    stat_row[2] = jnp.zeros_like(tops[0])
    for part in range(2):
        level = jnp.exp(tops[part] - stat_row[0])
        for n in range(1, 3):
            stat_row[n] += part_row[part, n] * level
        part_row[part, 0] = level

    owner = lax.rem(iota((seq_count, STRIDE), 0), tiles) == iota((seq_count, STRIDE), 1) // TILE
    code_row = lax.rem(iota((STRIDE, HEAD_DIM), 0), TILE)
    code_row = lax.rem(code_row, 2) * HALF + code_row // 2
    pick_lane = iota((STRIDE, HEAD_DIM), 1)
    code_col = lax.rem(iota((HEAD_DIM, STRIDE), 1), TILE)
    code_col = lax.rem(code_col, 2) * HALF + code_col // 2
    pick_row = iota((HEAD_DIM, STRIDE), 0)

    coded = jnp.zeros((seq_count, HEAD_DIM), F32)
    for n in range(3):
        values = jnp.broadcast_to(
            stat_row[n][:, None, :], (heads, tiles, STRIDE)
        ).reshape(seq_count, STRIDE)
        select = (pick_lane == code_row + n * PAIRS).astype(F32)
        coded = coded + dot_exact(jnp.where(owner, values, 0.0), select)
    stat_snd[:, 0, :] = coded
    stat_rcv[s] = stat_snd[s]

    @pl.loop(1, seq_count, unroll=UNROLL)
    def _(i):
        send(stat_snd, stat_rcv, 2, i)

    whole(gsnd, grcv, 1).wait_recv()
    sort_classes([lambda these: grcv[these]], 3)
    for p in range(PAIRS):
        pg = dot_nt(pair_of(2, p), pair_of(3, p))
        class_pg[p] = pg
        class_row[2 * PAIRS + p : 2 * PAIRS + p + 1, :] = jnp.sum(
            class_e[p] * pg, axis=0, keepdims=True
        )
    columns = class_row[...].T
    small = iota((seq_count, HEAD_DIM), 1) < HALF
    cstat_snd[:, 0, :] = jnp.where(
        small, columns[:seq_count], pltpu.roll(columns[seq_count:], HALF, 1)
    )
    cstat_rcv[s] = cstat_snd[s]

    @pl.loop(1, seq_count, unroll=UNROLL)
    def _(i):
        send(cstat_snd, cstat_rcv, 3, i)

    whole(stat_snd, stat_rcv, 2).wait_recv()
    band = stat_rcv[:, 0, :]
    band_row = jnp.concatenate([band, pltpu.roll(band, HEAD_DIM - HALF, 1)], axis=0).T
    for p in range(PAIRS):
        factor, delta = combine(
            *(class_row[n * PAIRS + p : n * PAIRS + p + 1, :] for n in range(3)),
            *(band_row[n * PAIRS + p : n * PAIRS + p + 1, :] for n in range(3)),
        )
        probs = class_e[p] * factor
        sgrad = (probs * (class_pg[p] - delta)).astype(BF16)
        for j, value in enumerate(
            (
                dot_tn(sgrad, pair_of(1, p)) * SCALE,
                dot_nn(sgrad, pair_of(0, p)) * SCALE,
                dot_nn(probs.astype(BF16), pair_of(3, p)),
            )
        ):
            class_grad[j, 2 * p : 2 * p + 2] = value.astype(BF16).reshape(
                2, seq_count, HEAD_DIM
            )
    for c in range(chunks):
        these = slice(c * TILE, (c + 1) * TILE)
        mixed = jnp.concatenate(
            [class_grad[j, :, these, :].reshape(STRIDE, HEAD_DIM) for j in range(3)], axis=1
        )
        sorted_rows = dot_nn(swap, mixed).astype(BF16)
        for j in range(3):
            grad_snd[these, j] = sorted_rows[:, j * HEAD_DIM : (j + 1) * HEAD_DIM].reshape(
                TILE, TILE, HEAD_DIM
            )
    grad_rcv[s] = grad_snd[s]

    @pl.loop(1, EARLY, unroll=UNROLL)
    def _(i):
        send(grad_snd, grad_rcv, 4, i)

    whole(cstat_snd, cstat_rcv, 3).wait_recv()
    got = cstat_rcv[:, 0, :]
    for n in range(3):
        select = (pick_row == code_col + n * PAIRS).astype(F32)
        cstat_row[n] = jnp.sum(
            jnp.where(owner, dot_exact(got, select), 0.0).reshape(heads, tiles, STRIDE), axis=1
        )

    def band_prev(h):
        factor, delta = combine(
            *(stat_row[n, h : h + 1, :] for n in range(3)),
            *(cstat_row[n, h : h + 1, :] for n in range(3)),
        )
        stat_row[0, h : h + 1, :] = factor
        stat_row[1, h : h + 1, :] = delta
        probs = e_prev[h] * (factor * part_row[1, 0, h : h + 1, :])
        sgrad = (probs * (pg_prev[h] - delta)).astype(BF16)
        back_snd[h, 0] = (dot_nn(sgrad, q_ref[h]) * SCALE).astype(BF16)
        back_snd[h, 1] = dot_nn(probs.astype(BF16), g_home[:, head_lanes(h)]).astype(BF16)
        for j in range(2):
            back_hop((h, j))
        acc[0, h] = dot_tn(sgrad, halo[h, 0])

    def band_own(h):
        factor, delta = (stat_row[n, h : h + 1, :] for n in range(2))
        probs = e_diag[h] * (factor * part_row[0, 0, h : h + 1, :])
        sgrad = (probs * (pg_diag[h] - delta)).astype(BF16)
        acc[0, h] = (acc[0, h] + dot_tn(sgrad, kv_ref[h, 0])) * SCALE
        acc[1, h] = dot_nn(sgrad, q_ref[h]) * SCALE
        acc[2, h] = dot_nn(probs.astype(BF16), g_home[:, head_lanes(h)])

    for h in range(direct, heads):
        band_prev(h)

    @pl.loop(EARLY, seq_count, unroll=UNROLL)
    def _(i):
        send(grad_snd, grad_rcv, 4, i)

    for h in range(direct):
        band_prev(h)
    for h in range(heads):
        band_own(h)
        for at in passed[h * len(passed) // heads : (h + 1) * len(passed) // heads]:
            back_pass(at)

    whole(grad_snd, grad_rcv, 4).wait_recv()
    for j in range(3):
        for h in range(heads):
            value = acc[j, h] + grad_rcv[h * tiles : (h + 1) * tiles, j].reshape(
                STRIDE, HEAD_DIM
            ).astype(F32)
            if j == 0:
                out_ref[0, :, head_lanes(h)] = value.astype(BF16)
            else:
                acc[j, h] = value
    back_all.wait_recv()
    for h in range(heads):
        for j in range(2):
            out_ref[1 + j, :, head_lanes(h)] = (acc[1 + j, h] + back_rcv[h, j].astype(F32)).astype(BF16)

    for copy in g_copies:
        copy.wait_send()
    halo_all.wait_send()
    for index, buffers in enumerate(
        ((snd, rcv), (gsnd, grcv), (stat_snd, stat_rcv), (cstat_snd, cstat_rcv), (grad_snd, grad_rcv))
    ):
        whole(*buffers, index).wait_send()
    back_all.wait_send()

    def sent(src, dst, send, recv):
        return hop_all(src, dst.at[pl.ds(0, direct)], send, recv)

    @pl.when(even)
    def _():
        sent(relay, halo, pass_send_sem.at[0], halo_recv_sem).wait_send()

    @pl.when(odd)
    def _():
        sent(back_relay, back_rcv, pass_send_sem.at[1], back_recv_sem).wait_send()


def per_device(queries, keys, values, out_grad):
    length, width = queries.shape
    seq_count = lax.axis_size("seq")
    head_count = lax.axis_size("head")
    heads = width // HEAD_DIM
    assert length == STRIDE and seq_count * TILE == STRIDE * heads and seq_count * 2 == HEAD_DIM
    vmem = pl.BlockSpec(memory_space=pltpu.VMEM)
    far = pl.BlockSpec(memory_space=pltpu.HBM)
    tile = (TILE, HEAD_DIM)
    pair = 2 * seq_count
    grads = pl.pallas_call(
        functools.partial(kernel, seq_count, head_count),
        out_shape=pltpu.VMEM((3,) + queries.shape, BF16),
        in_specs=[far] * 4,
        out_specs=vmem,
        scratch_shapes=[
            pltpu.VMEM((heads, length, HEAD_DIM), BF16),
            pltpu.VMEM((heads, 2, length, HEAD_DIM), BF16),
            pltpu.VMEM(out_grad.shape, BF16),
            pltpu.VMEM((length, width), BF16),
            pltpu.VMEM((heads, 2, length, HEAD_DIM), BF16),
            pltpu.VMEM((heads // 2, 2, length, HEAD_DIM), BF16),
            pltpu.VMEM((heads, 2, length, HEAD_DIM), BF16),
            pltpu.VMEM((heads, 2, length, HEAD_DIM), BF16),
            pltpu.VMEM((heads // 2, 2, length, HEAD_DIM), BF16),
            pltpu.VMEM((seq_count, 3) + tile, BF16),
            pltpu.VMEM((seq_count, 3) + tile, BF16),
            pltpu.VMEM((seq_count,) + tile, BF16),
            pltpu.VMEM((seq_count,) + tile, BF16),
            pltpu.VMEM((seq_count, 1, HEAD_DIM), F32),
            pltpu.VMEM((seq_count, 1, HEAD_DIM), F32),
            pltpu.VMEM((seq_count, 1, HEAD_DIM), F32),
            pltpu.VMEM((seq_count, 1, HEAD_DIM), F32),
            pltpu.VMEM((seq_count, 3) + tile, BF16),
            pltpu.VMEM((seq_count, 3) + tile, BF16),
            pltpu.VMEM((4, TILE, seq_count, HEAD_DIM), BF16),
            pltpu.VMEM((3, TILE, seq_count, HEAD_DIM), BF16),
            pltpu.VMEM((PAIRS, pair, pair), F32),
            pltpu.VMEM((PAIRS, pair, pair), F32),
            pltpu.VMEM((HEAD_DIM, HEAD_DIM), F32),
            pltpu.VMEM((heads, STRIDE, STRIDE), F32),
            pltpu.VMEM((heads, STRIDE, STRIDE), F32),
            pltpu.VMEM((heads, STRIDE, STRIDE), F32),
            pltpu.VMEM((heads, STRIDE, STRIDE), F32),
            pltpu.VMEM((2, 3, heads, STRIDE), F32),
            pltpu.VMEM((3, heads, STRIDE), F32),
            pltpu.VMEM((3, heads, STRIDE), F32),
            pltpu.VMEM((3, heads, length, HEAD_DIM), F32),
            pltpu.SemaphoreType.DMA((1 + 3 * heads,)),
            pltpu.SemaphoreType.DMA((head_count,)),
            pltpu.SemaphoreType.DMA((head_count,)),
            pltpu.SemaphoreType.DMA,
            pltpu.SemaphoreType.DMA,
            pltpu.SemaphoreType.DMA((heads // 2, 2)),
            pltpu.SemaphoreType.DMA,
            pltpu.SemaphoreType.DMA,
            pltpu.SemaphoreType.DMA((heads // 2, 2)),
            pltpu.SemaphoreType.DMA((2,)),
            pltpu.SemaphoreType.DMA((5,)),
            pltpu.SemaphoreType.DMA((5,)),
        ],
        compiler_params=pltpu.CompilerParams(
            collective_id=0, has_side_effects=True, vmem_limit_bytes=62 * 2**20
        ),
    )(queries, keys, values, out_grad)
    return grads[0], grads[1], grads[2]


def solution(mesh):
    return jax.shard_map(
        per_device,
        mesh=mesh,
        in_specs=(P("seq", "head"), P("seq", "head"), P("seq", "head"), P(("seq", "head"), None)),
        out_specs=(P("seq", "head"), P("seq", "head"), P("seq", "head")),
        check_vma=False,
    )
```

```python
import functools

import jax
import jax.numpy as jnp
from jax import lax
from jax.experimental import pallas as pl
from jax.experimental.pallas import tpu as pltpu
from jax.sharding import PartitionSpec as P

HEAD_DIM = 128
STRIDE = 256
TILE = 16
PAIRS = TILE // 2
HALF = 32
NEG_LARGE = -1e30
SCALE = HEAD_DIM**-0.5
EARLY = 37
UNROLL = 9
MESH = pl.DeviceIdType.MESH
F32 = jnp.float32
BF16 = jnp.bfloat16


def dot_nt(a, b):
    return lax.dot_general(a, b, (((1,), (1,)), ((), ())), preferred_element_type=F32)


def dot_nn(a, b):
    return lax.dot_general(a, b, (((1,), (0,)), ((), ())), preferred_element_type=F32)


def dot_tn(a, b):
    return lax.dot_general(a, b, (((0,), (0,)), ((), ())), preferred_element_type=F32)


def dot_exact(a, b):
    return lax.dot_general(
        a, b, (((1,), (0,)), ((), ())),
        preferred_element_type=F32, precision=lax.Precision.HIGHEST,
    )


def iota(shape, axis):
    return lax.broadcasted_iota(jnp.int32, shape, axis)


def combine(top, total, weighted, other_top, other_total, other_weighted):
    peak = jnp.maximum(top, other_top)
    mine, theirs = jnp.exp(top - peak), jnp.exp(other_top - peak)
    inverse = 1.0 / (total * mine + other_total * theirs)
    return mine * inverse, (weighted * mine + other_weighted * theirs) * inverse


def kernel(
    seq_count, head_count,
    q_hbm, k_hbm, v_hbm, og_hbm,
    out_ref,
    q_ref, kv_ref, og_ref, g_home, halo, relay, back_snd, back_rcv, back_relay,
    snd, rcv, gsnd, grcv, stat_snd, stat_rcv, cstat_snd, cstat_rcv, grad_snd, grad_rcv,
    classes, class_grad, class_e, class_pg, class_row,
    e_diag, e_prev, pg_diag, pg_prev, part_row, stat_row, cstat_row, acc,
    load_sem, g_send_sem, g_recv_sem, halo_send_sem, halo_recv_sem, relay_sem, back_send_sem, back_recv_sem, back_relay_sem,
    pass_send_sem, send_sem, recv_sem,
):
    s = lax.axis_index("seq")
    hd = lax.axis_index("head")
    others = seq_count - 1
    heads = q_ref.shape[0]
    width = heads * HEAD_DIM
    tiles = STRIDE // TILE
    chunks = seq_count // TILE
    after = lax.rem(s + 1, seq_count)
    part = og_ref.shape[0]

    def head_lanes(h):
        return slice(h * HEAD_DIM, (h + 1) * HEAD_DIM)

    loads = [pltpu.make_async_copy(og_hbm, og_ref, load_sem.at[0])]
    for h in range(heads):
        for j, (src, dst) in enumerate(
            ((q_hbm, q_ref.at[h]), (k_hbm, kv_ref.at[h, 0]), (v_hbm, kv_ref.at[h, 1]))
        ):
            loads.append(
                pltpu.make_async_copy(src.at[:, head_lanes(h)], dst, load_sem.at[1 + 3 * h + j])
            )
    for load in loads:
        load.start()

    barrier = pltpu.get_barrier_semaphore()

    @pl.loop(1, seq_count, unroll=UNROLL)
    def _(i):
        pl.semaphore_signal(
            barrier, inc=1, device_id=(lax.rem(s + i, seq_count), hd), device_id_type=MESH
        )

    @pl.loop(1, head_count)
    def _(i):
        pl.semaphore_signal(
            barrier, inc=1, device_id=(s, lax.rem(hd + i, head_count)), device_id_type=MESH
        )

    for load in loads:
        load.wait()
    for h in range(heads):
        for j, ref in enumerate((q_ref.at[h], kv_ref.at[h, 0], kv_ref.at[h, 1])):
            snd[h * tiles : (h + 1) * tiles, j] = ref[...].reshape(tiles, TILE, HEAD_DIM)
    rcv[s] = snd[s]
    own_rows = pl.ds(pl.multiple_of(hd * part, part), part)
    g_home[own_rows, :] = og_ref[:, pl.ds(pl.multiple_of(hd * width, width), width)]

    pl.semaphore_wait(barrier, others + head_count - 1)

    def send(src, dst, index, i):
        peer = lax.rem(s + i, seq_count)
        pltpu.make_async_remote_copy(
            src_ref=src.at[peer],
            dst_ref=dst.at[s],
            send_sem=send_sem.at[index],
            recv_sem=recv_sem.at[index],
            device_id=(peer, hd),
            device_id_type=MESH,
        ).start()

    def whole(src, dst, index):
        return pltpu.make_async_remote_copy(
            src_ref=src.at[pl.ds(0, others)],
            dst_ref=dst.at[pl.ds(0, others)],
            send_sem=send_sem.at[index],
            recv_sem=recv_sem.at[index],
            device_id=(after, hd),
            device_id_type=MESH,
        )

    odd = lax.rem(s, 2) == 1
    even = lax.rem(s, 2) == 0
    direct = heads // 2

    def hop(src, dst, at, send, recv, distance):
        return pltpu.make_async_remote_copy(
            src_ref=src.at[at],
            dst_ref=dst.at[at],
            send_sem=send,
            recv_sem=recv,
            device_id=(lax.rem(s + distance + seq_count, seq_count), hd),
            device_id_type=MESH,
        )

    def hop_relay(src, dst, at, send, recv, distance, to_relay):
        there = (at[0] - direct, at[1])
        return pltpu.make_async_remote_copy(
            src_ref=src.at[at] if to_relay else src.at[there],
            dst_ref=dst.at[there] if to_relay else dst.at[at],
            send_sem=send,
            recv_sem=recv,
            device_id=(lax.rem(s + distance + seq_count, seq_count), hd),
            device_id_type=MESH,
        )

    def halo_hop(at):
        straight = hop(kv_ref, halo, at, halo_send_sem, halo_recv_sem, 1)
        if at[0] < direct:
            straight.start()
            return

        @pl.when(even)
        def _():
            straight.start()

        @pl.when(odd)
        def _():
            halo_to_relay(at).start()

    def halo_to_relay(at):
        sem = relay_sem.at[at[0] - direct, at[1]]
        return hop_relay(kv_ref, relay, at, halo_send_sem, sem, -1, True)

    def halo_pass(at):
        @pl.when(even)
        def _():
            halo_to_relay(at).wait_recv()
            hop_relay(relay, halo, at, pass_send_sem.at[0], halo_recv_sem, 2, False).start()

    def back_hop(at):
        straight = hop(back_snd, back_rcv, at, back_send_sem, back_recv_sem, -1)
        if at[0] < direct:
            straight.start()
            return

        @pl.when(odd)
        def _():
            straight.start()

        @pl.when(even)
        def _():
            back_to_relay(at).start()

    def back_to_relay(at):
        sem = back_relay_sem.at[at[0] - direct, at[1]]
        return hop_relay(back_snd, back_relay, at, back_send_sem, sem, 1, True)

    def back_pass(at):
        @pl.when(odd)
        def _():
            back_to_relay(at).wait_recv()
            hop_relay(back_relay, back_rcv, at, pass_send_sem.at[1], back_recv_sem, -2, False).start()

    def hop_all(src, dst, send, recv):
        return pltpu.make_async_remote_copy(
            src_ref=src, dst_ref=dst, send_sem=send, recv_sem=recv,
            device_id=(after, hd), device_id_type=MESH,
        )

    passed = [(h, j) for h in range(direct, heads) for j in range(2)]
    kept = [(h, j) for h in range(direct) for j in range(2)]
    halo_all = hop_all(kv_ref, halo, halo_send_sem, halo_recv_sem)
    back_all = hop_all(back_snd, back_rcv, back_send_sem, back_recv_sem)

    g_copies = []
    for i in range(1, head_count):
        peer = lax.rem(hd + i, head_count)
        copy = pltpu.make_async_remote_copy(
            src_ref=og_ref.at[:, pl.ds(pl.multiple_of(peer * width, width), width)],
            dst_ref=g_home.at[own_rows, :],
            send_sem=g_send_sem.at[i],
            recv_sem=g_recv_sem.at[i],
            device_id=(s, peer),
            device_id_type=MESH,
        )
        copy.start()
        g_copies.append(copy)

    blocks = passed + kept
    share = seq_count // len(blocks)
    for n, at in enumerate(blocks):
        halo_hop(at)

        @pl.loop(max(1, n * share), (n + 1) * share, unroll=True)
        def _(i):
            send(snd, rcv, 0, i)

    for at in passed[:2]:
        halo_pass(at)

    for copy in g_copies:
        copy.wait_recv()
    for h in range(heads):
        gsnd[h * tiles : (h + 1) * tiles] = g_home[
            :, h * HEAD_DIM : (h + 1) * HEAD_DIM
        ].reshape(tiles, TILE, HEAD_DIM)

    @pl.loop(1, seq_count, unroll=UNROLL)
    def _(i):
        send(gsnd, grcv, 1, i)

    grcv[s] = gsnd[s]

    row = iota((STRIDE, STRIDE), 0)
    col = iota((STRIDE, STRIDE), 1)

    def band_part(h, keys, values, mask, e_part, pg_part, part):
        sc = jnp.where(mask, dot_nt(keys, q_ref[h]) * SCALE, NEG_LARGE)
        top = jnp.max(sc, axis=0, keepdims=True)
        ex = jnp.exp(sc - top)
        pg = dot_nt(values, g_home[:, head_lanes(h)])
        e_part[h], pg_part[h] = ex, pg
        total = jnp.sum(ex, axis=0, keepdims=True)
        weighted = jnp.sum(ex * pg, axis=0, keepdims=True)
        for n, value in enumerate((top, total, weighted)):
            part_row[part, n, h : h + 1, :] = value

    for h in range(heads):
        band_part(h, kv_ref[h, 0], kv_ref[h, 1], row <= col, e_diag, pg_diag, 0)
    for at in passed[2:]:
        halo_pass(at)

    swap_row = iota((STRIDE, STRIDE), 0)
    swap_col = iota((STRIDE, STRIDE), 1)
    swap = (
        (swap_row // TILE == lax.rem(swap_col, TILE))
        & (lax.rem(swap_row, TILE) == swap_col // TILE)
    ).astype(BF16)

    whole(snd, rcv, 0).wait_recv()

    def sort_classes(blocks, first):
        for c in range(chunks):
            these = slice(c * TILE, (c + 1) * TILE)
            mixed = jnp.concatenate(
                [block(these).reshape(STRIDE, HEAD_DIM) for block in blocks], axis=1
            )
            sorted_rows = dot_nn(swap, mixed).astype(BF16)
            for j in range(len(blocks)):
                classes[first + j, :, these, :] = sorted_rows[
                    :, j * HEAD_DIM : (j + 1) * HEAD_DIM
                ].reshape(TILE, TILE, HEAD_DIM)

    sort_classes([lambda these, j=j: rcv[these, j] for j in range(3)], 0)

    pair = 2 * seq_count
    prow = iota((pair, pair), 0)
    pcol = iota((pair, pair), 1)
    allowed = ((prow < seq_count) == (pcol < seq_count)) & (prow < pcol)

    def pair_of(j, p):
        return classes[j, 2 * p : 2 * p + 2].reshape(pair, HEAD_DIM)

    class_row[...] = jnp.zeros_like(class_row)
    for p in range(PAIRS):
        sc = jnp.where(allowed, dot_nt(pair_of(1, p), pair_of(0, p)) * SCALE, NEG_LARGE)
        top = jnp.max(sc, axis=0, keepdims=True)
        ec = jnp.where(allowed, jnp.exp(sc - top), 0.0)
        class_e[p] = ec
        class_row[p : p + 1, :] = top
        class_row[PAIRS + p : PAIRS + p + 1, :] = jnp.sum(ec, axis=0, keepdims=True)

    halo_all.wait_recv()
    for h in range(heads):
        band_part(h, halo[h, 0], halo[h, 1], (row > col) & (s > 0), e_prev, pg_prev, 1)
    tops = [part_row[part, 0] for part in range(2)]
    stat_row[0] = jnp.maximum(*tops)
    stat_row[1] = jnp.zeros_like(tops[0])
    stat_row[2] = jnp.zeros_like(tops[0])
    for part in range(2):
        level = jnp.exp(tops[part] - stat_row[0])
        for n in range(1, 3):
            stat_row[n] += part_row[part, n] * level
        part_row[part, 0] = level

    owner = lax.rem(iota((seq_count, STRIDE), 0), tiles) == iota((seq_count, STRIDE), 1) // TILE
    code_row = lax.rem(iota((STRIDE, HEAD_DIM), 0), TILE)
    code_row = lax.rem(code_row, 2) * HALF + code_row // 2
    pick_lane = iota((STRIDE, HEAD_DIM), 1)
    code_col = lax.rem(iota((HEAD_DIM, STRIDE), 1), TILE)
    code_col = lax.rem(code_col, 2) * HALF + code_col // 2
    pick_row = iota((HEAD_DIM, STRIDE), 0)

    coded = jnp.zeros((seq_count, HEAD_DIM), F32)
    for n in range(3):
        values = jnp.broadcast_to(
            stat_row[n][:, None, :], (heads, tiles, STRIDE)
        ).reshape(seq_count, STRIDE)
        select = (pick_lane == code_row + n * PAIRS).astype(F32)
        coded = coded + dot_exact(jnp.where(owner, values, 0.0), select)
    stat_snd[:, 0, :] = coded
    stat_rcv[s] = stat_snd[s]

    @pl.loop(1, seq_count, unroll=UNROLL)
    def _(i):
        send(stat_snd, stat_rcv, 2, i)

    whole(gsnd, grcv, 1).wait_recv()
    sort_classes([lambda these: grcv[these]], 3)
    for p in range(PAIRS):
        pg = dot_nt(pair_of(2, p), pair_of(3, p))
        class_pg[p] = pg
        class_row[2 * PAIRS + p : 2 * PAIRS + p + 1, :] = jnp.sum(
            class_e[p] * pg, axis=0, keepdims=True
        )
    columns = class_row[...].T
    small = iota((seq_count, HEAD_DIM), 1) < HALF
    cstat_snd[:, 0, :] = jnp.where(
        small, columns[:seq_count], pltpu.roll(columns[seq_count:], HALF, 1)
    )
    cstat_rcv[s] = cstat_snd[s]

    @pl.loop(1, seq_count, unroll=UNROLL)
    def _(i):
        send(cstat_snd, cstat_rcv, 3, i)

    whole(stat_snd, stat_rcv, 2).wait_recv()
    band = stat_rcv[:, 0, :]
    band_row = jnp.concatenate([band, pltpu.roll(band, HEAD_DIM - HALF, 1)], axis=0).T
    for p in range(PAIRS):
        factor, delta = combine(
            *(class_row[n * PAIRS + p : n * PAIRS + p + 1, :] for n in range(3)),
            *(band_row[n * PAIRS + p : n * PAIRS + p + 1, :] for n in range(3)),
        )
        probs = class_e[p] * factor
        sgrad = (probs * (class_pg[p] - delta)).astype(BF16)
        for j, value in enumerate(
            (
                dot_tn(sgrad, pair_of(1, p)) * SCALE,
                dot_nn(sgrad, pair_of(0, p)) * SCALE,
                dot_nn(probs.astype(BF16), pair_of(3, p)),
            )
        ):
            class_grad[j, 2 * p : 2 * p + 2] = value.astype(BF16).reshape(
                2, seq_count, HEAD_DIM
            )
    for c in range(chunks):
        these = slice(c * TILE, (c + 1) * TILE)
        mixed = jnp.concatenate(
            [class_grad[j, :, these, :].reshape(STRIDE, HEAD_DIM) for j in range(3)], axis=1
        )
        sorted_rows = dot_nn(swap, mixed).astype(BF16)
        for j in range(3):
            grad_snd[these, j] = sorted_rows[:, j * HEAD_DIM : (j + 1) * HEAD_DIM].reshape(
                TILE, TILE, HEAD_DIM
            )
    grad_rcv[s] = grad_snd[s]

    @pl.loop(1, EARLY, unroll=UNROLL)
    def _(i):
        send(grad_snd, grad_rcv, 4, i)

    whole(cstat_snd, cstat_rcv, 3).wait_recv()
    got = cstat_rcv[:, 0, :]
    for n in range(3):
        select = (pick_row == code_col + n * PAIRS).astype(F32)
        cstat_row[n] = jnp.sum(
            jnp.where(owner, dot_exact(got, select), 0.0).reshape(heads, tiles, STRIDE), axis=1
        )

    def band_prev(h):
        factor, delta = combine(
            *(stat_row[n, h : h + 1, :] for n in range(3)),
            *(cstat_row[n, h : h + 1, :] for n in range(3)),
        )
        stat_row[0, h : h + 1, :] = factor
        stat_row[1, h : h + 1, :] = delta
        probs = e_prev[h] * (factor * part_row[1, 0, h : h + 1, :])
        sgrad = (probs * (pg_prev[h] - delta)).astype(BF16)
        back_snd[h, 0] = (dot_nn(sgrad, q_ref[h]) * SCALE).astype(BF16)
        back_snd[h, 1] = dot_nn(probs.astype(BF16), g_home[:, head_lanes(h)]).astype(BF16)
        for j in range(2):
            back_hop((h, j))
        acc[0, h] = dot_tn(sgrad, halo[h, 0])

    def band_own(h):
        factor, delta = (stat_row[n, h : h + 1, :] for n in range(2))
        probs = e_diag[h] * (factor * part_row[0, 0, h : h + 1, :])
        sgrad = (probs * (pg_diag[h] - delta)).astype(BF16)
        acc[0, h] = (acc[0, h] + dot_tn(sgrad, kv_ref[h, 0])) * SCALE
        acc[1, h] = dot_nn(sgrad, q_ref[h]) * SCALE
        acc[2, h] = dot_nn(probs.astype(BF16), g_home[:, head_lanes(h)])

    for h in range(direct, heads):
        band_prev(h)

    @pl.loop(EARLY, seq_count, unroll=UNROLL)
    def _(i):
        send(grad_snd, grad_rcv, 4, i)

    for h in range(direct):
        band_prev(h)
    for at in passed:
        back_pass(at)
    for h in range(heads):
        band_own(h)

    whole(grad_snd, grad_rcv, 4).wait_recv()
    for j in range(3):
        for h in range(heads):
            value = acc[j, h] + grad_rcv[h * tiles : (h + 1) * tiles, j].reshape(
                STRIDE, HEAD_DIM
            ).astype(F32)
            if j == 0:
                out_ref[0, :, head_lanes(h)] = value.astype(BF16)
            else:
                acc[j, h] = value
    back_all.wait_recv()
    for h in range(heads):
        for j in range(2):
            out_ref[1 + j, :, head_lanes(h)] = (acc[1 + j, h] + back_rcv[h, j].astype(F32)).astype(BF16)

    for copy in g_copies:
        copy.wait_send()
    halo_all.wait_send()
    for index, buffers in enumerate(
        ((snd, rcv), (gsnd, grcv), (stat_snd, stat_rcv), (cstat_snd, cstat_rcv), (grad_snd, grad_rcv))
    ):
        whole(*buffers, index).wait_send()
    back_all.wait_send()

    def sent(src, dst, send, recv):
        return hop_all(src, dst.at[pl.ds(0, direct)], send, recv)

    @pl.when(even)
    def _():
        sent(relay, halo, pass_send_sem.at[0], halo_recv_sem).wait_send()

    @pl.when(odd)
    def _():
        sent(back_relay, back_rcv, pass_send_sem.at[1], back_recv_sem).wait_send()


def per_device(queries, keys, values, out_grad):
    length, width = queries.shape
    seq_count = lax.axis_size("seq")
    head_count = lax.axis_size("head")
    heads = width // HEAD_DIM
    assert length == STRIDE and seq_count * TILE == STRIDE * heads and seq_count * 2 == HEAD_DIM
    vmem = pl.BlockSpec(memory_space=pltpu.VMEM)
    far = pl.BlockSpec(memory_space=pltpu.HBM)
    tile = (TILE, HEAD_DIM)
    pair = 2 * seq_count
    grads = pl.pallas_call(
        functools.partial(kernel, seq_count, head_count),
        out_shape=pltpu.VMEM((3,) + queries.shape, BF16),
        in_specs=[far] * 4,
        out_specs=vmem,
        scratch_shapes=[
            pltpu.VMEM((heads, length, HEAD_DIM), BF16),
            pltpu.VMEM((heads, 2, length, HEAD_DIM), BF16),
            pltpu.VMEM(out_grad.shape, BF16),
            pltpu.VMEM((length, width), BF16),
            pltpu.VMEM((heads, 2, length, HEAD_DIM), BF16),
            pltpu.VMEM((heads // 2, 2, length, HEAD_DIM), BF16),
            pltpu.VMEM((heads, 2, length, HEAD_DIM), BF16),
            pltpu.VMEM((heads, 2, length, HEAD_DIM), BF16),
            pltpu.VMEM((heads // 2, 2, length, HEAD_DIM), BF16),
            pltpu.VMEM((seq_count, 3) + tile, BF16),
            pltpu.VMEM((seq_count, 3) + tile, BF16),
            pltpu.VMEM((seq_count,) + tile, BF16),
            pltpu.VMEM((seq_count,) + tile, BF16),
            pltpu.VMEM((seq_count, 1, HEAD_DIM), F32),
            pltpu.VMEM((seq_count, 1, HEAD_DIM), F32),
            pltpu.VMEM((seq_count, 1, HEAD_DIM), F32),
            pltpu.VMEM((seq_count, 1, HEAD_DIM), F32),
            pltpu.VMEM((seq_count, 3) + tile, BF16),
            pltpu.VMEM((seq_count, 3) + tile, BF16),
            pltpu.VMEM((4, TILE, seq_count, HEAD_DIM), BF16),
            pltpu.VMEM((3, TILE, seq_count, HEAD_DIM), BF16),
            pltpu.VMEM((PAIRS, pair, pair), F32),
            pltpu.VMEM((PAIRS, pair, pair), F32),
            pltpu.VMEM((HEAD_DIM, HEAD_DIM), F32),
            pltpu.VMEM((heads, STRIDE, STRIDE), F32),
            pltpu.VMEM((heads, STRIDE, STRIDE), F32),
            pltpu.VMEM((heads, STRIDE, STRIDE), F32),
            pltpu.VMEM((heads, STRIDE, STRIDE), F32),
            pltpu.VMEM((2, 3, heads, STRIDE), F32),
            pltpu.VMEM((3, heads, STRIDE), F32),
            pltpu.VMEM((3, heads, STRIDE), F32),
            pltpu.VMEM((3, heads, length, HEAD_DIM), F32),
            pltpu.SemaphoreType.DMA((1 + 3 * heads,)),
            pltpu.SemaphoreType.DMA((head_count,)),
            pltpu.SemaphoreType.DMA((head_count,)),
            pltpu.SemaphoreType.DMA,
            pltpu.SemaphoreType.DMA,
            pltpu.SemaphoreType.DMA((heads // 2, 2)),
            pltpu.SemaphoreType.DMA,
            pltpu.SemaphoreType.DMA,
            pltpu.SemaphoreType.DMA((heads // 2, 2)),
            pltpu.SemaphoreType.DMA((2,)),
            pltpu.SemaphoreType.DMA((5,)),
            pltpu.SemaphoreType.DMA((5,)),
        ],
        compiler_params=pltpu.CompilerParams(
            collective_id=0, has_side_effects=True, vmem_limit_bytes=62 * 2**20
        ),
    )(queries, keys, values, out_grad)
    return grads[0], grads[1], grads[2]


def solution(mesh):
    return jax.shard_map(
        per_device,
        mesh=mesh,
        in_specs=(P("seq", "head"), P("seq", "head"), P("seq", "head"), P(("seq", "head"), None)),
        out_specs=(P("seq", "head"), P("seq", "head"), P("seq", "head")),
        check_vma=False,
    )
```

```python
import functools

import jax
import jax.numpy as jnp
from jax import lax
from jax.experimental import pallas as pl
from jax.experimental.pallas import tpu as pltpu
from jax.sharding import PartitionSpec as P

HEAD_DIM = 128
STRIDE = 256
TILE = 16
PAIRS = TILE // 2
HALF = 32
NEG_LARGE = -1e30
SCALE = HEAD_DIM**-0.5
EARLY = 37
UNROLL = 9
MESH = pl.DeviceIdType.MESH
F32 = jnp.float32
BF16 = jnp.bfloat16


def dot_nt(a, b):
    return lax.dot_general(a, b, (((1,), (1,)), ((), ())), preferred_element_type=F32)


def dot_nn(a, b):
    return lax.dot_general(a, b, (((1,), (0,)), ((), ())), preferred_element_type=F32)


def dot_tn(a, b):
    return lax.dot_general(a, b, (((0,), (0,)), ((), ())), preferred_element_type=F32)


def dot_exact(a, b):
    return lax.dot_general(
        a, b, (((1,), (0,)), ((), ())),
        preferred_element_type=F32, precision=lax.Precision.HIGHEST,
    )


def iota(shape, axis):
    return lax.broadcasted_iota(jnp.int32, shape, axis)


def combine(top, total, weighted, other_top, other_total, other_weighted):
    peak = jnp.maximum(top, other_top)
    mine, theirs = jnp.exp(top - peak), jnp.exp(other_top - peak)
    inverse = 1.0 / (total * mine + other_total * theirs)
    return mine * inverse, (weighted * mine + other_weighted * theirs) * inverse


def kernel(
    seq_count, head_count,
    q_hbm, k_hbm, v_hbm, og_hbm,
    out_ref,
    q_ref, kv_ref, og_ref, g_home, halo, relay, back_snd, back_rcv, back_relay,
    snd, rcv, gsnd, grcv, stat_snd, stat_rcv, cstat_snd, cstat_rcv, grad_snd, grad_rcv,
    classes, class_grad, class_e, class_pg, class_row,
    e_diag, e_prev, pg_diag, pg_prev, part_row, stat_row, cstat_row, acc,
    load_sem, g_send_sem, g_recv_sem, halo_send_sem, halo_recv_sem, relay_sem, back_send_sem, back_recv_sem, back_relay_sem,
    pass_send_sem, send_sem, recv_sem,
):
    s = lax.axis_index("seq")
    hd = lax.axis_index("head")
    others = seq_count - 1
    heads = q_ref.shape[0]
    width = heads * HEAD_DIM
    tiles = STRIDE // TILE
    chunks = seq_count // TILE
    after = lax.rem(s + 1, seq_count)
    part = og_ref.shape[0]

    def head_lanes(h):
        return slice(h * HEAD_DIM, (h + 1) * HEAD_DIM)

    loads = [pltpu.make_async_copy(og_hbm, og_ref, load_sem.at[0])]
    for h in range(heads):
        for j, (src, dst) in enumerate(
            ((q_hbm, q_ref.at[h]), (k_hbm, kv_ref.at[h, 0]), (v_hbm, kv_ref.at[h, 1]))
        ):
            loads.append(
                pltpu.make_async_copy(src.at[:, head_lanes(h)], dst, load_sem.at[1 + 3 * h + j])
            )
    for load in loads:
        load.start()

    barrier = pltpu.get_barrier_semaphore()

    @pl.loop(1, seq_count, unroll=UNROLL)
    def _(i):
        pl.semaphore_signal(
            barrier, inc=1, device_id=(lax.rem(s + i, seq_count), hd), device_id_type=MESH
        )

    @pl.loop(1, head_count)
    def _(i):
        pl.semaphore_signal(
            barrier, inc=1, device_id=(s, lax.rem(hd + i, head_count)), device_id_type=MESH
        )

    for load in loads:
        load.wait()
    for h in range(heads):
        for j, ref in enumerate((q_ref.at[h], kv_ref.at[h, 0], kv_ref.at[h, 1])):
            snd[h * tiles : (h + 1) * tiles, j] = ref[...].reshape(tiles, TILE, HEAD_DIM)
    rcv[s] = snd[s]
    own_rows = pl.ds(pl.multiple_of(hd * part, part), part)
    g_home[own_rows, :] = og_ref[:, pl.ds(pl.multiple_of(hd * width, width), width)]

    pl.semaphore_wait(barrier, others + head_count - 1)

    def send(src, dst, index, i):
        peer = lax.rem(s + i, seq_count)
        pltpu.make_async_remote_copy(
            src_ref=src.at[peer],
            dst_ref=dst.at[s],
            send_sem=send_sem.at[index],
            recv_sem=recv_sem.at[index],
            device_id=(peer, hd),
            device_id_type=MESH,
        ).start()

    def whole(src, dst, index):
        return pltpu.make_async_remote_copy(
            src_ref=src.at[pl.ds(0, others)],
            dst_ref=dst.at[pl.ds(0, others)],
            send_sem=send_sem.at[index],
            recv_sem=recv_sem.at[index],
            device_id=(after, hd),
            device_id_type=MESH,
        )

    odd = lax.rem(s, 2) == 1
    even = lax.rem(s, 2) == 0
    direct = heads // 2

    def hop(src, dst, at, send, recv, distance):
        return pltpu.make_async_remote_copy(
            src_ref=src.at[at],
            dst_ref=dst.at[at],
            send_sem=send,
            recv_sem=recv,
            device_id=(lax.rem(s + distance + seq_count, seq_count), hd),
            device_id_type=MESH,
        )

    def hop_relay(src, dst, at, send, recv, distance, to_relay):
        there = (at[0] - direct, at[1])
        return pltpu.make_async_remote_copy(
            src_ref=src.at[at] if to_relay else src.at[there],
            dst_ref=dst.at[there] if to_relay else dst.at[at],
            send_sem=send,
            recv_sem=recv,
            device_id=(lax.rem(s + distance + seq_count, seq_count), hd),
            device_id_type=MESH,
        )

    def halo_hop(at):
        straight = hop(kv_ref, halo, at, halo_send_sem, halo_recv_sem, 1)
        if at[0] < direct:
            straight.start()
            return

        @pl.when(even)
        def _():
            straight.start()

        @pl.when(odd)
        def _():
            halo_to_relay(at).start()

    def halo_to_relay(at):
        sem = relay_sem.at[at[0] - direct, at[1]]
        return hop_relay(kv_ref, relay, at, halo_send_sem, sem, -1, True)

    def halo_pass(at):
        @pl.when(even)
        def _():
            halo_to_relay(at).wait_recv()
            hop_relay(relay, halo, at, pass_send_sem.at[0], halo_recv_sem, 2, False).start()

    def back_hop(at):
        straight = hop(back_snd, back_rcv, at, back_send_sem, back_recv_sem, -1)
        if at[0] < direct:
            straight.start()
            return

        @pl.when(odd)
        def _():
            straight.start()

        @pl.when(even)
        def _():
            back_to_relay(at).start()

    def back_to_relay(at):
        sem = back_relay_sem.at[at[0] - direct, at[1]]
        return hop_relay(back_snd, back_relay, at, back_send_sem, sem, 1, True)

    def back_pass(at):
        @pl.when(odd)
        def _():
            back_to_relay(at).wait_recv()
            hop_relay(back_relay, back_rcv, at, pass_send_sem.at[1], back_recv_sem, -2, False).start()

    def hop_all(src, dst, send, recv):
        return pltpu.make_async_remote_copy(
            src_ref=src, dst_ref=dst, send_sem=send, recv_sem=recv,
            device_id=(after, hd), device_id_type=MESH,
        )

    passed = [(h, j) for h in range(direct, heads) for j in range(2)]
    kept = [(h, j) for h in range(direct) for j in range(2)]
    halo_all = hop_all(kv_ref, halo, halo_send_sem, halo_recv_sem)
    back_all = hop_all(back_snd, back_rcv, back_send_sem, back_recv_sem)

    g_copies = []
    for i in range(1, head_count):
        peer = lax.rem(hd + i, head_count)
        copy = pltpu.make_async_remote_copy(
            src_ref=og_ref.at[:, pl.ds(pl.multiple_of(peer * width, width), width)],
            dst_ref=g_home.at[own_rows, :],
            send_sem=g_send_sem.at[i],
            recv_sem=g_recv_sem.at[i],
            device_id=(s, peer),
            device_id_type=MESH,
        )
        copy.start()
        g_copies.append(copy)

    blocks = passed + kept
    share = seq_count // len(blocks)
    for n, at in enumerate(blocks):
        halo_hop(at)

        @pl.loop(max(1, n * share), (n + 1) * share, unroll=True)
        def _(i):
            send(snd, rcv, 0, i)

    for at in passed[:2]:
        halo_pass(at)

    for copy in g_copies:
        copy.wait_recv()
    for h in range(heads):
        gsnd[h * tiles : (h + 1) * tiles] = g_home[
            :, h * HEAD_DIM : (h + 1) * HEAD_DIM
        ].reshape(tiles, TILE, HEAD_DIM)

    @pl.loop(1, seq_count, unroll=UNROLL)
    def _(i):
        send(gsnd, grcv, 1, i)

    grcv[s] = gsnd[s]

    row = iota((STRIDE, STRIDE), 0)
    col = iota((STRIDE, STRIDE), 1)

    def band_part(h, keys, values, mask, e_part, pg_part, part):
        sc = jnp.where(mask, dot_nt(keys, q_ref[h]) * SCALE, NEG_LARGE)
        top = jnp.max(sc, axis=0, keepdims=True)
        ex = jnp.exp(sc - top)
        pg = dot_nt(values, g_home[:, head_lanes(h)])
        e_part[h], pg_part[h] = ex, pg
        total = jnp.sum(ex, axis=0, keepdims=True)
        weighted = jnp.sum(ex * pg, axis=0, keepdims=True)
        for n, value in enumerate((top, total, weighted)):
            part_row[part, n, h : h + 1, :] = value

    for h in range(heads):
        band_part(h, kv_ref[h, 0], kv_ref[h, 1], row <= col, e_diag, pg_diag, 0)
    for at in passed[2:]:
        halo_pass(at)

    swap_row = iota((STRIDE, STRIDE), 0)
    swap_col = iota((STRIDE, STRIDE), 1)
    swap = (
        (swap_row // TILE == lax.rem(swap_col, TILE))
        & (lax.rem(swap_row, TILE) == swap_col // TILE)
    ).astype(BF16)

    whole(snd, rcv, 0).wait_recv()

    def sort_classes(blocks, first):
        for c in range(chunks):
            these = slice(c * TILE, (c + 1) * TILE)
            mixed = jnp.concatenate(
                [block(these).reshape(STRIDE, HEAD_DIM) for block in blocks], axis=1
            )
            sorted_rows = dot_nn(swap, mixed).astype(BF16)
            for j in range(len(blocks)):
                classes[first + j, :, these, :] = sorted_rows[
                    :, j * HEAD_DIM : (j + 1) * HEAD_DIM
                ].reshape(TILE, TILE, HEAD_DIM)

    sort_classes([lambda these, j=j: rcv[these, j] for j in range(3)], 0)

    pair = 2 * seq_count
    prow = iota((pair, pair), 0)
    pcol = iota((pair, pair), 1)
    allowed = ((prow < seq_count) == (pcol < seq_count)) & (prow < pcol)

    def pair_of(j, p):
        return classes[j, 2 * p : 2 * p + 2].reshape(pair, HEAD_DIM)

    class_row[...] = jnp.zeros_like(class_row)
    for p in range(PAIRS):
        sc = jnp.where(allowed, dot_nt(pair_of(1, p), pair_of(0, p)) * SCALE, NEG_LARGE)
        top = jnp.max(sc, axis=0, keepdims=True)
        ec = jnp.where(allowed, jnp.exp(sc - top), 0.0)
        class_e[p] = ec
        class_row[p : p + 1, :] = top
        class_row[PAIRS + p : PAIRS + p + 1, :] = jnp.sum(ec, axis=0, keepdims=True)

    halo_all.wait_recv()
    for h in range(heads):
        band_part(h, halo[h, 0], halo[h, 1], (row > col) & (s > 0), e_prev, pg_prev, 1)
    tops = [part_row[part, 0] for part in range(2)]
    stat_row[0] = jnp.maximum(*tops)
    stat_row[1] = jnp.zeros_like(tops[0])
    stat_row[2] = jnp.zeros_like(tops[0])
    for part in range(2):
        level = jnp.exp(tops[part] - stat_row[0])
        for n in range(1, 3):
            stat_row[n] += part_row[part, n] * level
        part_row[part, 0] = level

    owner = lax.rem(iota((seq_count, STRIDE), 0), tiles) == iota((seq_count, STRIDE), 1) // TILE
    code_row = lax.rem(iota((STRIDE, HEAD_DIM), 0), TILE)
    code_row = lax.rem(code_row, 2) * HALF + code_row // 2
    pick_lane = iota((STRIDE, HEAD_DIM), 1)
    code_col = lax.rem(iota((HEAD_DIM, STRIDE), 1), TILE)
    code_col = lax.rem(code_col, 2) * HALF + code_col // 2
    pick_row = iota((HEAD_DIM, STRIDE), 0)

    coded = jnp.zeros((seq_count, HEAD_DIM), F32)
    for n in range(3):
        values = jnp.broadcast_to(
            stat_row[n][:, None, :], (heads, tiles, STRIDE)
        ).reshape(seq_count, STRIDE)
        select = (pick_lane == code_row + n * PAIRS).astype(F32)
        coded = coded + dot_exact(jnp.where(owner, values, 0.0), select)
    stat_snd[:, 0, :] = coded
    stat_rcv[s] = stat_snd[s]

    @pl.loop(1, seq_count, unroll=UNROLL)
    def _(i):
        send(stat_snd, stat_rcv, 2, i)

    whole(gsnd, grcv, 1).wait_recv()
    sort_classes([lambda these: grcv[these]], 3)
    for p in range(PAIRS):
        pg = dot_nt(pair_of(2, p), pair_of(3, p))
        class_pg[p] = pg
        class_row[2 * PAIRS + p : 2 * PAIRS + p + 1, :] = jnp.sum(
            class_e[p] * pg, axis=0, keepdims=True
        )
    columns = class_row[...].T
    small = iota((seq_count, HEAD_DIM), 1) < HALF
    cstat_snd[:, 0, :] = jnp.where(
        small, columns[:seq_count], pltpu.roll(columns[seq_count:], HALF, 1)
    )
    cstat_rcv[s] = cstat_snd[s]

    @pl.loop(1, seq_count, unroll=True)
    def _(i):
        send(cstat_snd, cstat_rcv, 3, i)

    whole(stat_snd, stat_rcv, 2).wait_recv()
    band = stat_rcv[:, 0, :]
    band_row = jnp.concatenate([band, pltpu.roll(band, HEAD_DIM - HALF, 1)], axis=0).T
    for p in range(PAIRS):
        factor, delta = combine(
            *(class_row[n * PAIRS + p : n * PAIRS + p + 1, :] for n in range(3)),
            *(band_row[n * PAIRS + p : n * PAIRS + p + 1, :] for n in range(3)),
        )
        probs = class_e[p] * factor
        sgrad = (probs * (class_pg[p] - delta)).astype(BF16)
        for j, value in enumerate(
            (
                dot_tn(sgrad, pair_of(1, p)) * SCALE,
                dot_nn(sgrad, pair_of(0, p)) * SCALE,
                dot_nn(probs.astype(BF16), pair_of(3, p)),
            )
        ):
            class_grad[j, 2 * p : 2 * p + 2] = value.astype(BF16).reshape(
                2, seq_count, HEAD_DIM
            )
    for c in range(chunks):
        these = slice(c * TILE, (c + 1) * TILE)
        mixed = jnp.concatenate(
            [class_grad[j, :, these, :].reshape(STRIDE, HEAD_DIM) for j in range(3)], axis=1
        )
        sorted_rows = dot_nn(swap, mixed).astype(BF16)
        for j in range(3):
            grad_snd[these, j] = sorted_rows[:, j * HEAD_DIM : (j + 1) * HEAD_DIM].reshape(
                TILE, TILE, HEAD_DIM
            )
    grad_rcv[s] = grad_snd[s]

    @pl.loop(1, EARLY, unroll=UNROLL)
    def _(i):
        send(grad_snd, grad_rcv, 4, i)

    whole(cstat_snd, cstat_rcv, 3).wait_recv()
    got = cstat_rcv[:, 0, :]
    for n in range(3):
        select = (pick_row == code_col + n * PAIRS).astype(F32)
        cstat_row[n] = jnp.sum(
            jnp.where(owner, dot_exact(got, select), 0.0).reshape(heads, tiles, STRIDE), axis=1
        )

    def band_prev(h):
        factor, delta = combine(
            *(stat_row[n, h : h + 1, :] for n in range(3)),
            *(cstat_row[n, h : h + 1, :] for n in range(3)),
        )
        stat_row[0, h : h + 1, :] = factor
        stat_row[1, h : h + 1, :] = delta
        probs = e_prev[h] * (factor * part_row[1, 0, h : h + 1, :])
        sgrad = (probs * (pg_prev[h] - delta)).astype(BF16)
        back_snd[h, 0] = (dot_nn(sgrad, q_ref[h]) * SCALE).astype(BF16)
        back_snd[h, 1] = dot_nn(probs.astype(BF16), g_home[:, head_lanes(h)]).astype(BF16)
        for j in range(2):
            back_hop((h, j))
        acc[0, h] = dot_tn(sgrad, halo[h, 0])

    def band_own(h):
        factor, delta = (stat_row[n, h : h + 1, :] for n in range(2))
        probs = e_diag[h] * (factor * part_row[0, 0, h : h + 1, :])
        sgrad = (probs * (pg_diag[h] - delta)).astype(BF16)
        acc[0, h] = (acc[0, h] + dot_tn(sgrad, kv_ref[h, 0])) * SCALE
        acc[1, h] = dot_nn(sgrad, q_ref[h]) * SCALE
        acc[2, h] = dot_nn(probs.astype(BF16), g_home[:, head_lanes(h)])

    for h in range(direct, heads):
        band_prev(h)

    @pl.loop(EARLY, seq_count, unroll=UNROLL)
    def _(i):
        send(grad_snd, grad_rcv, 4, i)

    for h in range(direct):
        band_prev(h)
    for at in passed:
        back_pass(at)
    for h in range(heads):
        band_own(h)

    whole(grad_snd, grad_rcv, 4).wait_recv()
    for j in range(3):
        for h in range(heads):
            value = acc[j, h] + grad_rcv[h * tiles : (h + 1) * tiles, j].reshape(
                STRIDE, HEAD_DIM
            ).astype(F32)
            if j == 0:
                out_ref[0, :, head_lanes(h)] = value.astype(BF16)
            else:
                acc[j, h] = value
    back_all.wait_recv()
    for h in range(heads):
        for j in range(2):
            out_ref[1 + j, :, head_lanes(h)] = (acc[1 + j, h] + back_rcv[h, j].astype(F32)).astype(BF16)

    for copy in g_copies:
        copy.wait_send()
    halo_all.wait_send()
    for index, buffers in enumerate(
        ((snd, rcv), (gsnd, grcv), (stat_snd, stat_rcv), (cstat_snd, cstat_rcv), (grad_snd, grad_rcv))
    ):
        whole(*buffers, index).wait_send()
    back_all.wait_send()

    def sent(src, dst, send, recv):
        return hop_all(src, dst.at[pl.ds(0, direct)], send, recv)

    @pl.when(even)
    def _():
        sent(relay, halo, pass_send_sem.at[0], halo_recv_sem).wait_send()

    @pl.when(odd)
    def _():
        sent(back_relay, back_rcv, pass_send_sem.at[1], back_recv_sem).wait_send()


def per_device(queries, keys, values, out_grad):
    length, width = queries.shape
    seq_count = lax.axis_size("seq")
    head_count = lax.axis_size("head")
    heads = width // HEAD_DIM
    assert length == STRIDE and seq_count * TILE == STRIDE * heads and seq_count * 2 == HEAD_DIM
    vmem = pl.BlockSpec(memory_space=pltpu.VMEM)
    far = pl.BlockSpec(memory_space=pltpu.HBM)
    tile = (TILE, HEAD_DIM)
    pair = 2 * seq_count
    grads = pl.pallas_call(
        functools.partial(kernel, seq_count, head_count),
        out_shape=pltpu.VMEM((3,) + queries.shape, BF16),
        in_specs=[far] * 4,
        out_specs=vmem,
        scratch_shapes=[
            pltpu.VMEM((heads, length, HEAD_DIM), BF16),
            pltpu.VMEM((heads, 2, length, HEAD_DIM), BF16),
            pltpu.VMEM(out_grad.shape, BF16),
            pltpu.VMEM((length, width), BF16),
            pltpu.VMEM((heads, 2, length, HEAD_DIM), BF16),
            pltpu.VMEM((heads // 2, 2, length, HEAD_DIM), BF16),
            pltpu.VMEM((heads, 2, length, HEAD_DIM), BF16),
            pltpu.VMEM((heads, 2, length, HEAD_DIM), BF16),
            pltpu.VMEM((heads // 2, 2, length, HEAD_DIM), BF16),
            pltpu.VMEM((seq_count, 3) + tile, BF16),
            pltpu.VMEM((seq_count, 3) + tile, BF16),
            pltpu.VMEM((seq_count,) + tile, BF16),
            pltpu.VMEM((seq_count,) + tile, BF16),
            pltpu.VMEM((seq_count, 1, HEAD_DIM), F32),
            pltpu.VMEM((seq_count, 1, HEAD_DIM), F32),
            pltpu.VMEM((seq_count, 1, HEAD_DIM), F32),
            pltpu.VMEM((seq_count, 1, HEAD_DIM), F32),
            pltpu.VMEM((seq_count, 3) + tile, BF16),
            pltpu.VMEM((seq_count, 3) + tile, BF16),
            pltpu.VMEM((4, TILE, seq_count, HEAD_DIM), BF16),
            pltpu.VMEM((3, TILE, seq_count, HEAD_DIM), BF16),
            pltpu.VMEM((PAIRS, pair, pair), F32),
            pltpu.VMEM((PAIRS, pair, pair), F32),
            pltpu.VMEM((HEAD_DIM, HEAD_DIM), F32),
            pltpu.VMEM((heads, STRIDE, STRIDE), F32),
            pltpu.VMEM((heads, STRIDE, STRIDE), F32),
            pltpu.VMEM((heads, STRIDE, STRIDE), F32),
            pltpu.VMEM((heads, STRIDE, STRIDE), F32),
            pltpu.VMEM((2, 3, heads, STRIDE), F32),
            pltpu.VMEM((3, heads, STRIDE), F32),
            pltpu.VMEM((3, heads, STRIDE), F32),
            pltpu.VMEM((3, heads, length, HEAD_DIM), F32),
            pltpu.SemaphoreType.DMA((1 + 3 * heads,)),
            pltpu.SemaphoreType.DMA((head_count,)),
            pltpu.SemaphoreType.DMA((head_count,)),
            pltpu.SemaphoreType.DMA,
            pltpu.SemaphoreType.DMA,
            pltpu.SemaphoreType.DMA((heads // 2, 2)),
            pltpu.SemaphoreType.DMA,
            pltpu.SemaphoreType.DMA,
            pltpu.SemaphoreType.DMA((heads // 2, 2)),
            pltpu.SemaphoreType.DMA((2,)),
            pltpu.SemaphoreType.DMA((5,)),
            pltpu.SemaphoreType.DMA((5,)),
        ],
        compiler_params=pltpu.CompilerParams(
            collective_id=0, has_side_effects=True, vmem_limit_bytes=62 * 2**20
        ),
    )(queries, keys, values, out_grad)
    return grads[0], grads[1], grads[2]


def solution(mesh):
    return jax.shard_map(
        per_device,
        mesh=mesh,
        in_specs=(P("seq", "head"), P("seq", "head"), P("seq", "head"), P(("seq", "head"), None)),
        out_specs=(P("seq", "head"), P("seq", "head"), P("seq", "head")),
        check_vma=False,
    )
```
